32 devices in a mesh: row: 8 (over z, x), col: 4 (over y, core).
Axes of the slice: x: 2, y: 2, z: 4, core: 2. Of those that a mesh axis runs over, the one named last changes fastest.
Arguments:
- pixels: bfloat16 [128, 64, 768], P('row', 'col'), may hold values from -6 to 6
- conv_weight: bfloat16 [3, 3, 64, 128], replicated, may hold values from -0.25 to 0.25
- time_weight: bfloat16 [3, 16, 8, 8], replicated, may hold values from -1.25 to 1.25
- class_weight: bfloat16 [128, 20], replicated, may hold values from -0.5 to 0.5
- pixel_slot: int32 [128, 64], P('row', 'col'), may hold values from 0 to 63, as said below
- straddle_dir: int32 [8, 4, 32], P('row', 'col'), may hold values from 0 to 8, as said below
- straddle_slot: int32 [8, 4, 32], P('row', 'col'), may hold values from 0 to 31
- labels: int32 [8, 4, 32], P('row', 'col'), may hold values from 0 to 19
Outputs:
- input_grad: bfloat16 [128, 64, 768], P('row', 'col')
- conv_grad: float32 [3, 3, 64, 128], replicated
- time_grad: float32 [3, 16, 8, 8], replicated
- class_grad: float32 [128, 20], replicated
The draws below stay inside these ranges and needn't reach their ends.
Inputs may be any that keep to these rules, and one draw needn't show every extreme that they name: `pixel_slot`: below 32 a pixel is in the tile's own parcel of that number, from 32 on in its straddling entry of that number minus 32. Every index of a tile's list is held by at least one pixel of that tile. The owner of entry e of tile (r, c) is tile (r + q // 3 - 1, c + q % 3 - 1) with q = straddle_dir[r, c, e]; q is never 4 and the owner lies within the scene.
All inputs are finite; a program needn't handle non-finite values.
Results may differ from the reference program's by a relative error of at most 0.012.
Values may be sent and summed in bfloat16 or wider, within the bound.
A program may use at most 64 MiB of HBM per device.

```python
import jax
import jax.numpy as jnp
from jax import lax

HT = 16
WT = 16
DATES = 12
C_IN = 64
C_OUT = 128
GROUPS = 16
CLASSES = 20
P_OWN = 32
S_STR = 32
CPG = 8
NH = 128
NW = 64
PARCELS = 1024
N_ROW = 8
N_COL = 4


def draw_pixel_slot(key, part):
    row_tiles = NH // HT
    col_tiles = NW // WT
    slot_count = P_OWN + S_STR
    key_base = jax.random.fold_in(key, 11)
    key_rank = jax.random.fold_in(key, 12)
    base_slot = jax.random.randint(key_base, (row_tiles, col_tiles, HT * WT), 0, slot_count)
    local_index = jnp.arange(HT * WT, dtype=jnp.int32)
    scores = jax.random.randint(key_rank, (row_tiles, col_tiles, HT * WT), 0, 32768) * (HT * WT) + local_index
    ranking = jnp.argsort(jnp.argsort(scores, axis=-1), axis=-1)
    slot_map = jnp.where(ranking < slot_count, ranking, base_slot)
    slot_map = slot_map.reshape(row_tiles, col_tiles, HT, WT).transpose(0, 2, 1, 3).reshape(NH, NW)
    return slot_map.astype(jnp.int32)


def draw_straddle_dir(key, part):
    row_tiles = NH // HT
    col_tiles = NW // WT
    key_row = jax.random.fold_in(key, 21)
    key_col = jax.random.fold_in(key, 22)
    shape_out = (row_tiles, col_tiles, S_STR)
    row_step = jax.random.randint(key_row, shape_out, -1, 2)
    col_step = jax.random.randint(key_col, shape_out, -1, 2)
    tile_row = jnp.arange(row_tiles, dtype=jnp.int32)[:, None, None]
    tile_col = jnp.arange(col_tiles, dtype=jnp.int32)[None, :, None]
    row_step = jnp.where(tile_row + row_step < 0, 1, jnp.where(tile_row + row_step >= row_tiles, -1, row_step))
    col_step = jnp.where(tile_col + col_step < 0, 1, jnp.where(tile_col + col_step >= col_tiles, -1, col_step))
    itself = (row_step == 0) & (col_step == 0)
    col_step = jnp.where(itself, jnp.where(tile_col + 1 < col_tiles, 1, -1), col_step)
    return ((row_step + 1) * 3 + col_step + 1).astype(jnp.int32)


def with_ends(values, stream_key, smallest, largest):
    shape = values.shape
    index_at = [jax.random.randint(jax.random.fold_in(stream_key, axis), (), 0, shape[axis]) for axis in range(len(shape))]
    values = values.at[tuple(index_at)].set(smallest)
    longest = shape.index(max(shape))
    index_at[longest] = (index_at[longest] + 1) % shape[longest]
    return values.at[tuple(index_at)].set(largest)


def levels(rng, shape, split, low, largest):
    factor_of = 1.0
    for position, blocks in split:
        heights = jax.random.uniform(jax.random.fold_in(jax.random.fold_in(rng, 6), position), (blocks,), jnp.float32, low / len(split), largest / len(split))
        factor_of = factor_of * jnp.repeat(jnp.exp(heights), shape[position] // blocks).reshape((-1,) + (1,) * (len(shape) - 1 - position))
    return factor_of


def scatter_about(own_key, dims, spread, most, cuts=(), kind=jnp.bfloat16):
    factor_of = levels(own_key, dims, cuts, -0.22, 0.18) if cuts else 1.0
    values = jax.random.normal(own_key, dims, jnp.float32) * spread * factor_of
    return jnp.minimum(jnp.maximum(values, -most), most).astype(kind)


def setup_inputs(seed: int = 0) -> dict:
    key_list = jax.random.split(jax.random.key(seed), 9)
    pixels = scatter_about(key_list[0], (NH, NW, DATES * C_IN), 1.0, 6.0, ((0, 8), (1, 4)))
    conv_weight = scatter_about(key_list[1], (3, 3, C_IN, C_OUT), (9 * C_IN) ** -0.5, 0.25)
    time_weight = scatter_about(key_list[2], (3, GROUPS, CPG, CPG), (3 * CPG) ** -0.5, 1.25)
    class_weight = scatter_about(key_list[3], (C_OUT, CLASSES), C_OUT ** -0.5, 0.5)
    pixel_slot = draw_pixel_slot(jax.random.fold_in(key_list[8], 71), 0)
    straddle_dir = draw_straddle_dir(jax.random.fold_in(key_list[8], 71), 0)
    straddle_slot = with_ends(jax.random.randint(key_list[6], (N_ROW, N_COL, S_STR), 0, P_OWN), jax.random.fold_in(key_list[6], 1), 0, P_OWN - 1).astype(jnp.int32)
    labels = with_ends(jax.random.randint(key_list[7], (N_ROW, N_COL, P_OWN), 0, CLASSES), jax.random.fold_in(key_list[7], 1), 0, CLASSES - 1).astype(jnp.int32)
    return {"pixels": pixels, "conv_weight": conv_weight, "time_weight": time_weight, "class_weight": class_weight, "pixel_slot": pixel_slot, "straddle_dir": straddle_dir, "straddle_slot": straddle_slot, "labels": labels}


EPSILON = 1e-05
PRECISE = lax.Precision.HIGHEST

def silu_slope(value):
    sig = jax.nn.sigmoid(value)
    return sig * (1.0 + value * (1.0 - sig))

def spatial_conv(padded, conv_weight, out_rows, out_cols):
    running_sum = jnp.zeros((out_rows, out_cols, DATES, C_OUT), jnp.float32)
    for row_tap in range(3):
        for col_tap in range(3):
            window = padded[row_tap:row_tap + out_rows, col_tap:col_tap + out_cols].astype(jnp.float32)
            running_sum = running_sum + jnp.einsum('ijtc,cd->ijtd', window, conv_weight[row_tap, col_tap].astype(jnp.float32), precision=PRECISE)
    return running_sum

def temporal_conv(hidden, time_weight):
    band_rows, band_cols = (hidden.shape[0], hidden.shape[1])
    grouped = hidden.astype(jnp.float32).reshape(band_rows, band_cols, DATES, GROUPS, CPG)
    padded = jnp.pad(grouped, ((0, 0), (0, 0), (1, 1), (0, 0), (0, 0)))
    running_sum = jnp.zeros((band_rows, band_cols, DATES, GROUPS, CPG), jnp.float32)
    for time_tap in range(3):
        running_sum = running_sum + jnp.einsum('ijtgc,gcd->ijtgd', padded[:, :, time_tap:time_tap + DATES], time_weight[time_tap].astype(jnp.float32), precision=PRECISE)
    return running_sum.reshape(band_rows, band_cols, DATES, C_OUT)

def temporal_back(grad_mixed, time_weight):
    band_rows, band_cols = (grad_mixed.shape[0], grad_mixed.shape[1])
    grouped = grad_mixed.astype(jnp.float32).reshape(band_rows, band_cols, DATES, GROUPS, CPG)
    padded = jnp.pad(grouped, ((0, 0), (0, 0), (1, 1), (0, 0), (0, 0)))
    running_sum = jnp.zeros((band_rows, band_cols, DATES, GROUPS, CPG), jnp.float32)
    for time_tap in range(3):
        running_sum = running_sum + jnp.einsum('ijtgd,gcd->ijtgc', padded[:, :, 2 - time_tap:2 - time_tap + DATES], time_weight[time_tap].astype(jnp.float32), precision=PRECISE)
    return running_sum.reshape(band_rows, band_cols, DATES, C_OUT)

def temporal_weight_grad(hidden, grad_mixed):
    band_rows, band_cols = (hidden.shape[0], hidden.shape[1])
    grouped = hidden.astype(jnp.float32).reshape(band_rows, band_cols, DATES, GROUPS, CPG)
    padded = jnp.pad(grouped, ((0, 0), (0, 0), (1, 1), (0, 0), (0, 0)))
    grad_grouped = grad_mixed.astype(jnp.float32).reshape(band_rows, band_cols, DATES, GROUPS, CPG)
    taps = [jnp.einsum('ijtgc,ijtgd->gcd', padded[:, :, time_tap:time_tap + DATES], grad_grouped, precision=PRECISE) for time_tap in range(3)]
    return jnp.stack(taps)

def parcel_index(pixel_slot, straddle_dir, straddle_slot):
    tile_row = jnp.broadcast_to((jnp.arange(NH, dtype=jnp.int32) // HT)[:, None], (NH, NW))
    tile_col = jnp.broadcast_to((jnp.arange(NW, dtype=jnp.int32) // WT)[None, :], (NH, NW))
    home_tile = tile_row * N_COL + tile_col
    foreign = jnp.clip(pixel_slot - P_OWN, 0, S_STR - 1).astype(jnp.int32)
    direction = straddle_dir[tile_row, tile_col, foreign]
    owner_slot = straddle_slot[tile_row, tile_col, foreign]
    owner_tile = (tile_row + direction // 3 - 1) * N_COL + tile_col + direction % 3 - 1
    return jnp.where(pixel_slot < P_OWN, home_tile * P_OWN + pixel_slot, owner_tile * P_OWN + owner_slot).astype(jnp.int32)

def reference(pixels, conv_weight, time_weight, class_weight, pixel_slot, straddle_dir, straddle_slot, labels):
    padded_pixels = jnp.pad(pixels.reshape(NH, NW, DATES, C_IN), ((2, 2), (1, 1), (0, 0), (0, 0)))

    def forward_band(band_index):
        first_row = band_index * HT
        row_block = lax.dynamic_slice_in_dim(padded_pixels, first_row + 1, HT + 2, 0)
        pre_act = spatial_conv(row_block, conv_weight, HT, NW)
        hidden = jax.nn.silu(pre_act).astype(jnp.bfloat16)
        mixed_time = temporal_conv(hidden, time_weight)
        return lax.optimization_barrier(jnp.mean(jax.nn.silu(mixed_time), axis=2)).astype(jnp.bfloat16)
    embedded = lax.map(forward_band, jnp.arange(N_ROW, dtype=jnp.int32)).reshape(NH * NW, C_OUT)
    parcel_of = parcel_index(pixel_slot, straddle_dir, straddle_slot).reshape(NH * NW)
    parcel_sums = jax.ops.segment_sum(embedded.astype(jnp.float32), parcel_of, num_segments=PARCELS)
    centered = parcel_sums - lax.optimization_barrier(jnp.mean(parcel_sums, axis=-1, keepdims=True))
    variance = lax.optimization_barrier(jnp.mean(centered * centered, axis=-1, keepdims=True))
    inverse = lax.rsqrt(variance + EPSILON)
    normed = centered * inverse
    rounded = normed.astype(jnp.bfloat16)
    logits = jnp.dot(rounded, class_weight, preferred_element_type=jnp.float32)
    exp_logits = jnp.exp(logits)
    probability = exp_logits / lax.optimization_barrier(jnp.sum(exp_logits, axis=-1, keepdims=True))
    label_hot = (labels.reshape(PARCELS)[:, None] == jnp.arange(CLASSES, dtype=jnp.int32)[None, :]).astype(jnp.float32)
    grad_logits = (probability - label_hot) / PARCELS
    class_grad = jnp.dot(rounded.astype(jnp.float32).T, grad_logits, precision=PRECISE)
    grad_normed = jnp.dot(grad_logits, class_weight.astype(jnp.float32).T, precision=PRECISE)
    parcel_grad = (inverse * (grad_normed - lax.optimization_barrier(jnp.mean(grad_normed, axis=-1, keepdims=True)) - normed * lax.optimization_barrier(jnp.mean(grad_normed * normed, axis=-1, keepdims=True)))).astype(jnp.bfloat16)
    pixel_grad = jnp.take(parcel_grad, parcel_of, axis=0).reshape(NH, NW, C_OUT)
    padded_grad = jnp.pad(pixel_grad, ((1, 1), (0, 0), (0, 0)))

    def backward_band(running, band_index):
        conv_acc, time_acc = running
        first_row = band_index * HT
        row_block = lax.dynamic_slice_in_dim(padded_pixels, first_row, HT + 4, 0)
        pre_act = spatial_conv(row_block, conv_weight, HT + 2, NW)
        hidden = jax.nn.silu(pre_act).astype(jnp.bfloat16)
        mixed_time = temporal_conv(hidden, time_weight)
        grad_rows = lax.dynamic_slice_in_dim(padded_grad, first_row, HT + 2, 0)
        grad_mixed = ((grad_rows.astype(jnp.float32) / DATES)[:, :, None, :] * silu_slope(mixed_time)).astype(jnp.bfloat16)
        grad_hidden = temporal_back(grad_mixed, time_weight)
        grad_pre = (grad_hidden * silu_slope(pre_act)).astype(jnp.bfloat16)
        time_acc = time_acc + temporal_weight_grad(hidden[1:HT + 1], grad_mixed[1:HT + 1])
        own_block = row_block[1:HT + 3].astype(jnp.float32)
        grad_own = grad_pre[1:HT + 1].astype(jnp.float32)
        conv_taps = jnp.stack([jnp.stack([jnp.einsum('ijtc,ijtd->cd', own_block[row_tap:row_tap + HT, col_tap:col_tap + NW], grad_own, precision=PRECISE) for col_tap in range(3)]) for row_tap in range(3)])
        conv_acc = conv_acc + conv_taps
        first_keep = jnp.where(band_index == 0, 0.0, 1.0).astype(jnp.float32)
        last_keep = jnp.where(band_index == N_ROW - 1, 0.0, 1.0).astype(jnp.float32)
        row_keep = jnp.concatenate([first_keep[None], jnp.ones((HT,), jnp.float32), last_keep[None]])
        grad_masked = grad_pre.astype(jnp.float32) * row_keep[:, None, None, None]
        grad_padded = jnp.pad(grad_masked, ((0, 0), (1, 1), (0, 0), (0, 0)))
        band_grad = jnp.zeros((HT, NW, DATES, C_IN), jnp.float32)
        for row_tap in range(3):
            for col_tap in range(3):
                band_grad = band_grad + jnp.einsum('ijtd,cd->ijtc', grad_padded[2 - row_tap:2 - row_tap + HT, 2 - col_tap:2 - col_tap + NW], conv_weight[row_tap, col_tap].astype(jnp.float32), precision=PRECISE)
        return ((conv_acc, time_acc), band_grad.astype(jnp.bfloat16))
    initial = (jnp.zeros((3, 3, C_IN, C_OUT), jnp.float32), jnp.zeros((3, GROUPS, CPG, CPG), jnp.float32))
    (conv_grad, time_grad), bands = lax.scan(backward_band, initial, jnp.arange(N_ROW, dtype=jnp.int32))
    input_grad = bands.reshape(NH, NW, DATES * C_IN)
    return (input_grad, conv_grad, time_grad, class_grad)
```

```python
import functools

import jax
import jax.numpy as jnp
from jax import lax
from jax.experimental import pallas as pl
from jax.experimental.pallas import tpu as pltpu
from jax.sharding import PartitionSpec as P

DATES = 12
C_IN = 64
C_OUT = 128
GROUPS = 16
CLASSES = 20
P_OWN = 32
S_STR = 32
CPG = 8
EPSILON = 1e-05
PRECISE = lax.Precision.HIGHEST
MESH = pl.DeviceIdType.MESH
F32 = jnp.float32
BF16 = jnp.bfloat16

T = 16
PIX = T * T
PAIRS = DATES // 2
LX = DATES * C_IN
LG = DATES * C_OUT
SLOTS = 9 * P_OWN
CONV_ROWS = 9 * C_IN
SMALL_ROWS = 48
DIRS = [d for d in range(9) if d != 4]


def iota(shape, dim):
    return lax.broadcasted_iota(jnp.int32, shape, dim)


def dot(a, b, dims=((1,), (0,)), precision=None):
    return lax.dot_general(
        a, b, (dims, ((), ())), preferred_element_type=F32, precision=precision
    )


def sigmoid(v):
    return 0.5 * jnp.tanh(0.5 * v) + 0.5


def kernel(
    n_row,
    n_col,
    shard,
    x_ref,
    cw_ref,
    tw_ref,
    kw_ref,
    slot_ref,
    sdir_ref,
    sslot_ref,
    lab_ref,
    gx_ref,
    gcw_ref,
    gtw_ref,
    gkw_ref,
    xf,
    xs,
    xc,
    wf,
    wb,
    b4f,
    b4b,
    onehot,
    onehot_t,
    hid,
    gmix,
    hid_t,
    slope_pre,
    slope_mix,
    gpre,
    zs,
    zacc,
    col_send,
    col_recv,
    cor_send,
    cor_recv,
    sum_send,
    sum_recv,
    pgrad,
    beside,
    z_send,
    z_recv,
    part,
    rs_recv,
    bx_recv,
    final,
    px_ss,
    px_rs,
    ps_ss,
    ps_rs,
    pg_ss,
    pg_rs,
    gh_ss,
    gh_rs,
    zc_ss,
    zc_rs,
    rs_ss,
    rs_rs,
    bx_ss,
    bx_rs,
    ag_ss,
    ag_rs,
):
    row = lax.axis_index("row")
    col = lax.axis_index("col")
    n_a = 2 * n_col
    n_b = n_row // 2
    base = lax.div(row, 2)
    a_row = lax.rem(row, 2)
    a_me = a_row * n_col + col

    def a_dev(k):
        q = lax.rem(a_me + k, n_a)
        return q, (base * 2 + lax.div(q, n_col), lax.rem(q, n_col))

    def b_dev(k):
        return (lax.rem(base + k, n_b) * 2 + a_row, col)

    def neighbour(d):
        r = row + (d // 3 - 1)
        c = col + (d % 3 - 1)
        there = (r >= 0) & (r < n_row) & (c >= 0) & (c < n_col)
        return there, (r, c)

    xc[1, 0] = jnp.zeros((T, LX), BF16)
    xc[1, T + 1] = jnp.zeros((T, LX), BF16)
    gpre[0] = jnp.zeros((T, LG), BF16)
    gpre[T + 1] = jnp.zeros((T, LG), BF16)
    col_recv[...] = jnp.zeros(col_recv.shape, BF16)
    cor_recv[...] = jnp.zeros(cor_recv.shape, BF16)
    sum_recv[...] = jnp.zeros(sum_recv.shape, BF16)
    beside[...] = jnp.zeros(beside.shape, BF16)
    z_recv[...] = jnp.zeros(z_recv.shape, BF16)

    barrier = pltpu.get_barrier_semaphore()
    expected = n_a - 1 + n_b - 1
    for d in DIRS:
        there, dev = neighbour(d)
        expected = expected + there.astype(jnp.int32)

        @pl.when(there)
        def _():
            pl.semaphore_signal(barrier, inc=1, device_id=dev, device_id_type=MESH)

    for k in range(1, n_a):
        pl.semaphore_signal(barrier, inc=1, device_id=a_dev(k)[1], device_id_type=MESH)
    for k in range(1, n_b):
        pl.semaphore_signal(barrier, inc=1, device_id=b_dev(k), device_id_type=MESH)

    x_own = x_ref[...].astype(F32).reshape(PIX, LX)
    left, right = [], []
    for p in range(PAIRS):
        xf[p] = x_own[:, p * 128 : (p + 1) * 128]
        left.append(xf[p, pl.ds(0, T, stride=T), :])
        right.append(xf[p, pl.ds(T - 1, T, stride=T), :])
        col_send[0, :, p * 128 : (p + 1) * 128] = left[p].astype(BF16)
        col_send[1, :, p * 128 : (p + 1) * 128] = right[p].astype(BF16)
    which = iota((T, 128), 0)
    for corner, source, at in ((0, left, 0), (1, right, 0), (2, left, T - 1), (3, right, T - 1)):
        block = jnp.zeros((T, 128), F32)
        for p in range(PAIRS):
            piece = source[p][at : at + 1, :]
            block = jnp.where(which == p, jnp.broadcast_to(piece, (T, 128)), block)
        cor_send[corner] = block.astype(BF16)

    pl.semaphore_wait(barrier, expected)

    corner_of = {0: 0, 2: 1, 6: 2, 8: 3}

    def pixel_copy(d, dev):
        o = 8 - d
        if d in corner_of:
            src, dst = cor_send.at[corner_of[d]], cor_recv.at[corner_of[o]]
        elif d == 1:
            src, dst = x_ref.at[0], xc.at[1, T + 1]
        elif d == 7:
            src, dst = x_ref.at[T - 1], xc.at[1, 0]
        elif d == 3:
            src, dst = col_send.at[0], col_recv.at[1]
        else:
            src, dst = col_send.at[1], col_recv.at[0]
        return pltpu.make_async_remote_copy(
            src_ref=src,
            dst_ref=dst,
            send_sem=px_ss.at[d],
            recv_sem=px_rs.at[o],
            device_id=dev,
            device_id_type=MESH,
        )

    def sums_copy(d, dev):
        return pltpu.make_async_remote_copy(
            src_ref=sum_send.at[d],
            dst_ref=sum_recv.at[8 - d],
            send_sem=ps_ss.at[d],
            recv_sem=ps_rs.at[8 - d],
            device_id=dev,
            device_id_type=MESH,
        )

    def grad_copy(d, dev):
        return pltpu.make_async_remote_copy(
            src_ref=pgrad,
            dst_ref=beside.at[8 - d],
            send_sem=pg_ss.at[d],
            recv_sem=pg_rs.at[8 - d],
            device_id=dev,
            device_id_type=MESH,
        )

    def row_copy(d, dev):
        k = 0 if d == 1 else 1
        return pltpu.make_async_remote_copy(
            src_ref=gpre.at[1 if d == 1 else T],
            dst_ref=gpre.at[T + 1 if d == 1 else 0],
            send_sem=gh_ss.at[k],
            recv_sem=gh_rs.at[1 - k],
            device_id=dev,
            device_id_type=MESH,
        )

    def col_copy(d, dev):
        k = 0 if d == 3 else 1
        return pltpu.make_async_remote_copy(
            src_ref=z_send.at[k],
            dst_ref=z_recv.at[1 - k],
            send_sem=zc_ss.at[k],
            recv_sem=zc_rs.at[1 - k],
            device_id=dev,
            device_id_type=MESH,
        )

    def start_all(make, dirs):
        for d in dirs:
            there, dev = neighbour(d)

            @pl.when(there)
            def _():
                make(d, dev).start()

    def wait_recv_all(make, dirs):
        for d in dirs:
            there, dev = neighbour(d)

            @pl.when(there)
            def _():
                make(8 - d, dev).wait_recv()

    def wait_send_all(make, dirs):
        for d in dirs:
            there, dev = neighbour(d)

            @pl.when(there)
            def _():
                make(d, dev).wait_send()

    start_all(pixel_copy, DIRS)

    xc[1, 1 : T + 1] = x_ref[...]
    wf[...] = jnp.zeros(wf.shape, BF16)
    for r in range(3):
        for c in range(3):
            t = r * 3 + c
            w = cw_ref[r, c]
            wf[t * 128 : t * 128 + 64, 0:128] = w
            wf[t * 128 + 64 : t * 128 + 128, 128:256] = w
    for r in range(3):
        for slot_at, c in ((0, 0), (1, 2), (2, 1)):
            t = r * 3 + c
            block = wf[t * 128 : (t + 1) * 128, :].astype(F32)
            wb[r * 256 : (r + 1) * 256, slot_at * 128 : (slot_at + 1) * 128] = block.T.astype(BF16)
    same_group = lax.div(iota((128, 128), 0), CPG) == lax.div(iota((128, 128), 1), CPG)
    spread = (iota((CPG, 128), 0) == lax.rem(iota((CPG, 128), 1), CPG)).astype(F32)
    dense, dense_t = [], []
    for tap in range(3):
        compact = tw_ref[tap].astype(F32).reshape(128, CPG)
        d_tap = jnp.where(same_group, dot(compact, spread), 0.0)
        dense.append(d_tap.astype(BF16))
        dense_t.append(d_tap.T.astype(BF16))
    nothing = jnp.zeros((128, 128), BF16)
    for ref, (one, two, three) in ((b4f, dense), (b4b, dense_t[::-1])):
        for i, (lo, hi) in enumerate(((one, nothing), (two, one), (three, two), (nothing, three))):
            ref[i * 128 : (i + 1) * 128, 0:128] = lo
            ref[i * 128 : (i + 1) * 128, 128:256] = hi
    zero_side = jnp.zeros((PIX, 128), BF16)
    hid[:, 0:128] = zero_side
    hid[:, 128 + LG : 256 + LG] = zero_side
    gmix[:, 0:128] = zero_side
    gmix[:, 128 + LG : 256 + LG] = zero_side

    pick_row = (lax.div(iota((PIX, T), 0), T) == iota((PIX, T), 1)).astype(BF16)
    by_row = dot(pick_row, slot_ref[...].astype(F32).astype(BF16))
    at_col = lax.rem(iota((PIX, T), 0), T) == iota((PIX, T), 1)
    slot_of = jnp.sum(jnp.where(at_col, by_row, 0.0), axis=1, keepdims=True).astype(jnp.int32)
    in_own = (slot_of == iota((PIX, P_OWN), 1)).astype(BF16)
    in_str = (slot_of - P_OWN == iota((PIX, S_STR), 1)).astype(BF16)
    target = sdir_ref[0] * P_OWN + sslot_ref[0]
    sel_own = (iota((SLOTS, P_OWN), 0) == iota((SLOTS, P_OWN), 1) + 4 * P_OWN).astype(BF16)
    sel_str = (iota((SLOTS, S_STR), 0) == target).astype(BF16)
    onehot[...] = (
        dot(sel_own, in_own, ((1,), (1,))) + dot(sel_str, in_str, ((1,), (1,)))
    ).astype(BF16)
    onehot_t[...] = (
        dot(in_own, sel_own, ((1,), (1,))) + dot(in_str, sel_str, ((1,), (1,)))
    ).astype(BF16)

    for p in range(PAIRS):
        lanes = x_own[:, p * 128 : (p + 1) * 128]
        xs[0, p, T : T + PIX] = pltpu.roll(lanes, 1, 0)
        xs[1, p, T : T + PIX] = pltpu.roll(lanes, PIX - 1, 0)
    wait_recv_all(pixel_copy, DIRS)
    for halo in (0, T + 1):
        line = xc[1, halo].astype(F32)
        for p in range(PAIRS):
            lanes = line[:, p * 128 : (p + 1) * 128]
            xs[0, p, halo * T : (halo + 1) * T] = pltpu.roll(lanes, 1, 0)
            xs[1, p, halo * T : (halo + 1) * T] = pltpu.roll(lanes, T - 1, 0)
    for side, at in ((0, 0), (1, T - 1)):
        arrived = col_recv[side].astype(F32)
        top = cor_recv[side].astype(F32)
        bottom = cor_recv[2 + side].astype(F32)
        last = (T + 1) * T
        for p in range(PAIRS):
            lanes = slice(p * 128, (p + 1) * 128)
            xs[side, p, pl.ds(T + at, T, stride=T), :] = arrived[:, lanes]
            xs[side, p, at : at + 1, :] = top[p : p + 1, :]
            xs[side, p, last + at : last + at + 1, :] = bottom[p : p + 1, :]
            xc[2 * side, :, :, lanes] = xs[side, p].astype(BF16).reshape(T + 2, T, 128)

    def taps(p):
        return jnp.concatenate(
            [
                xc[c, r : r + T, :, p * 128 : (p + 1) * 128].reshape(PIX, 128)
                for r in range(3)
                for c in range(3)
            ],
            axis=1,
        )

    for p in range(PAIRS):
        pre = dot(taps(p), wf[...])
        sig = sigmoid(pre)
        act = pre * sig
        slope_pre[:, p * 256 : (p + 1) * 256] = sig + act * (1.0 - sig)
        hid[:, 128 + p * 256 : 128 + (p + 1) * 256] = act.astype(BF16)
    total = jnp.zeros((PIX, 256), F32)
    for p in range(PAIRS):
        mixed = dot(hid[:, p * 256 : p * 256 + 512], b4f[...])
        sig = sigmoid(mixed)
        act = mixed * sig
        slope_mix[:, p * 256 : (p + 1) * 256] = (sig + act * (1.0 - sig)) * (1.0 / DATES)
        total = total + act
    embedded = ((total[:, 0:128] + total[:, 128:256]) * (1.0 / DATES)).astype(BF16)
    outgoing = dot(onehot[...], embedded)
    for d in DIRS:
        sum_send[d] = outgoing[d * P_OWN : (d + 1) * P_OWN].astype(BF16)
    start_all(sums_copy, DIRS)
    sums = outgoing[4 * P_OWN : 5 * P_OWN]
    for p in range(PAIRS):
        hid_t[p * 256 : (p + 1) * 256, :] = hid[:, 128 + p * 256 : 128 + (p + 1) * 256].T
    wait_recv_all(sums_copy, DIRS)
    for d in DIRS:
        sums = sums + sum_recv[d].astype(F32)

    centered = sums - jnp.mean(sums, axis=-1, keepdims=True)
    inverse = lax.rsqrt(jnp.mean(centered * centered, axis=-1, keepdims=True) + EPSILON)
    normed = centered * inverse
    rounded = normed.astype(BF16)
    kw = kw_ref[...]
    logits = dot(rounded, kw)
    exps = jnp.exp(logits)
    prob = exps / jnp.sum(exps, axis=-1, keepdims=True)
    lab = lab_ref[0]
    lab_col = jnp.sum(
        jnp.where(iota((P_OWN, P_OWN), 0) == iota((P_OWN, P_OWN), 1), lab.astype(F32), 0.0),
        axis=1,
        keepdims=True,
    ).astype(jnp.int32)
    hot = (lab_col == iota((P_OWN, CLASSES), 1)).astype(F32)
    g_logits = (prob - hot) * (1.0 / (P_OWN * n_row * n_col))
    g_normed = dot(g_logits, kw.astype(F32), ((1,), (1,)), PRECISE)
    g_parcel = inverse * (
        g_normed
        - jnp.mean(g_normed, axis=-1, keepdims=True)
        - normed * jnp.mean(g_normed * normed, axis=-1, keepdims=True)
    )
    g_parcel = g_parcel.astype(BF16)
    pgrad[...] = g_parcel
    start_all(grad_copy, DIRS)
    beside[4] = g_parcel
    class_term = dot(g_logits, rounded.astype(F32), ((0,), (0,)), PRECISE)
    wait_recv_all(grad_copy, DIRS)

    pixel_grad = dot(onehot_t[...], beside[...].reshape(SLOTS, C_OUT))
    pixel_grad = jnp.concatenate([pixel_grad, pixel_grad], axis=1)
    for p in range(PAIRS):
        gmix[:, 128 + p * 256 : 128 + (p + 1) * 256] = (
            pixel_grad * slope_mix[:, p * 256 : (p + 1) * 256]
        ).astype(BF16)
    for p in range(PAIRS):
        g_hid = dot(gmix[:, p * 256 : p * 256 + 512], b4b[...])
        g_pre = (g_hid * slope_pre[:, p * 256 : (p + 1) * 256]).astype(BF16)
        gpre[1 : T + 1, :, p * 256 : (p + 1) * 256] = g_pre.reshape(T, T, 256)
    start_all(row_copy, (1, 7))

    conv_t = None
    for p in range(PAIRS):
        g_pair = gpre[1 : T + 1, :, p * 256 : (p + 1) * 256].reshape(PIX, 256)
        term = dot(g_pair, taps(p), ((0,), (0,)))
        conv_t = term if conv_t is None else conv_t + term
    low_half = iota((128, 128), 1) < C_IN
    for t in range(9):
        both = jnp.where(
            low_half,
            conv_t[0:128, t * 128 : (t + 1) * 128],
            conv_t[128:256, t * 128 : (t + 1) * 128],
        ).T
        part[t * 64 : (t + 1) * 64, :] = (both[0:64] + both[64:128]).astype(BF16)
    even = None
    for p in range(PAIRS):
        term = dot(
            hid_t[p * 256 : (p + 1) * 256, :], gmix[:, 128 + p * 256 : 128 + (p + 1) * 256]
        )
        even = term if even is None else even + term
    odd = None
    for p in range(PAIRS - 1):
        term = dot(
            hid_t[p * 256 + 128 : p * 256 + 384, :],
            gmix[:, 256 + p * 256 : 512 + p * 256],
        )
        odd = term if odd is None else odd + term
    time_taps = (
        even[0:128, 128:256] + odd[0:128, 128:256],
        even[0:128, 0:128] + even[128:256, 128:256],
        even[128:256, 0:128] + odd[128:256, 0:128],
    )
    small = [
        jnp.sum(jnp.where(same_group, tap, 0.0).reshape(GROUPS, CPG, 128), axis=0)
        for tap in time_taps
    ]
    small.append(class_term)
    small.append(jnp.zeros((SMALL_ROWS - 3 * CPG - CLASSES, 128), F32))
    part[CONV_ROWS : CONV_ROWS + SMALL_ROWS, :] = jnp.concatenate(small, axis=0).astype(BF16)

    def shard_at(q):
        return pl.ds(pl.multiple_of(q * shard, 16), shard)

    def rs_copy(k):
        q, dev = a_dev(k)
        return pltpu.make_async_remote_copy(
            src_ref=part.at[shard_at(q)],
            dst_ref=rs_recv.at[k],
            send_sem=rs_ss.at[k],
            recv_sem=rs_rs.at[k],
            device_id=dev,
            device_id_type=MESH,
        )

    def bx_copy(k):
        return pltpu.make_async_remote_copy(
            src_ref=bx_recv.at[base],
            dst_ref=bx_recv.at[base],
            send_sem=bx_ss.at[k],
            recv_sem=bx_rs.at[k],
            device_id=b_dev(k),
            device_id_type=MESH,
        )

    def ag_copy(k):
        return pltpu.make_async_remote_copy(
            src_ref=final.at[shard_at(a_me)],
            dst_ref=final.at[shard_at(a_me)],
            send_sem=ag_ss.at[k],
            recv_sem=ag_rs.at[k],
            device_id=a_dev(k)[1],
            device_id_type=MESH,
        )

    for k in range(1, n_a):
        rs_copy(k).start()

    wait_recv_all(row_copy, (1, 7))
    j_at = lax.rem(iota((PIX, 128), 0), T)
    for p in range(PAIRS):
        g_rows = jnp.concatenate(
            [
                gpre[2 - r : 2 - r + T, :, p * 256 : (p + 1) * 256].reshape(PIX, 256)
                for r in range(3)
            ],
            axis=1,
        )
        z = dot(g_rows, wb[...])
        zs[0] = z[:, 0:128]
        zs[1] = z[:, 128:256]
        z_send[0, :, p * 128 : (p + 1) * 128] = zs[0, pl.ds(0, T, stride=T), :].astype(BF16)
        z_send[1, :, p * 128 : (p + 1) * 128] = zs[1, pl.ds(T - 1, T, stride=T), :].astype(BF16)
        from_right = jnp.where(j_at == T - 1, 0.0, pltpu.roll(z[:, 0:128], PIX - 1, 0))
        from_left = jnp.where(j_at == 0, 0.0, pltpu.roll(z[:, 128:256], 1, 0))
        zacc[p] = z[:, 256:384] + from_right + from_left
    start_all(col_copy, (3, 5))

    mine = part[shard_at(a_me)].astype(F32)
    for k in range(1, n_a):
        rs_copy(k).wait_recv()
    for k in range(1, n_a):
        mine = mine + rs_recv[k].astype(F32)
    bx_recv[base] = mine.astype(BF16)
    for k in range(1, n_b):
        bx_copy(k).start()

    wait_recv_all(col_copy, (3, 5))
    for p in range(PAIRS):
        lanes = slice(p * 128, (p + 1) * 128)
        at_left = zacc[p, pl.ds(0, T, stride=T), :] + z_recv[0, :, lanes].astype(F32)
        zacc[p, pl.ds(0, T, stride=T), :] = at_left
        at_right = zacc[p, pl.ds(T - 1, T, stride=T), :] + z_recv[1, :, lanes].astype(F32)
        zacc[p, pl.ds(T - 1, T, stride=T), :] = at_right
        gx_ref[:, :, lanes] = zacc[p].astype(BF16).reshape(T, T, 128)

    for k in range(1, n_b):
        pltpu.make_async_remote_copy(
            src_ref=bx_recv.at[base],
            dst_ref=bx_recv.at[lax.rem(base + n_b - k, n_b)],
            send_sem=bx_ss.at[k],
            recv_sem=bx_rs.at[k],
            device_id=b_dev(k),
            device_id_type=MESH,
        ).wait_recv()
    whole = bx_recv[0].astype(F32)
    for g in range(1, n_b):
        whole = whole + bx_recv[g].astype(F32)
    final[shard_at(a_me)] = whole.astype(BF16)
    for k in range(1, n_a):
        ag_copy(k).start()
    wait_send_all(pixel_copy, DIRS)
    wait_send_all(sums_copy, DIRS)
    wait_send_all(grad_copy, DIRS)
    wait_send_all(row_copy, (1, 7))
    wait_send_all(col_copy, (3, 5))
    for k in range(1, n_a):
        rs_copy(k).wait_send()
    for k in range(1, n_b):
        bx_copy(k).wait_send()
    for k in range(1, n_a):
        q = lax.rem(a_me + n_a - k, n_a)
        pltpu.make_async_remote_copy(
            src_ref=final.at[shard_at(a_me)],
            dst_ref=final.at[shard_at(q)],
            send_sem=ag_ss.at[k],
            recv_sem=ag_rs.at[k],
            device_id=a_dev(k)[1],
            device_id_type=MESH,
        ).wait_recv()
    for t in range(9):
        gcw_ref[t // 3, t % 3] = final[t * 64 : (t + 1) * 64, :].astype(F32)
    small_sum = final[CONV_ROWS : CONV_ROWS + SMALL_ROWS, :].astype(F32)
    for tap in range(3):
        for g in range(GROUPS):
            gtw_ref[tap, g] = small_sum[tap * CPG : (tap + 1) * CPG, g * CPG : (g + 1) * CPG]
    class_rows = jnp.concatenate(
        [small_sum[3 * CPG : SMALL_ROWS], jnp.zeros((128 - SMALL_ROWS + 3 * CPG, 128), F32)], axis=0
    )
    gkw_ref[...] = class_rows.T[:, 0:CLASSES]
    for k in range(1, n_a):
        ag_copy(k).wait_send()


def per_device(n_row, n_col, *args):
    n_a = 2 * n_col
    n_b = n_row // 2
    rows = CONV_ROWS + SMALL_ROWS
    shard = -(-rows // (16 * n_a)) * 16
    total = shard * n_a
    vmem = pl.BlockSpec(memory_space=pltpu.VMEM)
    dma = pltpu.SemaphoreType.DMA
    return pl.pallas_call(
        functools.partial(kernel, n_row, n_col, shard),
        out_shape=(
            jax.ShapeDtypeStruct((T, T, LX), BF16),
            jax.ShapeDtypeStruct((3, 3, C_IN, C_OUT), F32),
            jax.ShapeDtypeStruct((3, GROUPS, CPG, CPG), F32),
            jax.ShapeDtypeStruct((C_OUT, CLASSES), F32),
        ),
        in_specs=[vmem] * 8,
        out_specs=(vmem,) * 4,
        scratch_shapes=[
            pltpu.VMEM((PAIRS, PIX, 128), F32),
            pltpu.VMEM((2, PAIRS, PIX + 2 * T, 128), F32),
            pltpu.VMEM((3, T + 2, T, LX), BF16),
            pltpu.VMEM((9 * 128, 256), BF16),
            pltpu.VMEM((3 * 256, 3 * 128), BF16),
            pltpu.VMEM((512, 256), BF16),
            pltpu.VMEM((512, 256), BF16),
            pltpu.VMEM((SLOTS, PIX), BF16),
            pltpu.VMEM((PIX, SLOTS), BF16),
            pltpu.VMEM((PIX, LG + 256), BF16),
            pltpu.VMEM((PIX, LG + 256), BF16),
            pltpu.VMEM((LG, PIX), BF16),
            pltpu.VMEM((PIX, LG), F32),
            pltpu.VMEM((PIX, LG), F32),
            pltpu.VMEM((T + 2, T, LG), BF16),
            pltpu.VMEM((2, PIX, 128), F32),
            pltpu.VMEM((PAIRS, PIX, 128), F32),
            pltpu.VMEM((2, T, LX), BF16),
            pltpu.VMEM((2, T, LX), BF16),
            pltpu.VMEM((4, T, 128), BF16),
            pltpu.VMEM((4, T, 128), BF16),
            pltpu.VMEM((9, P_OWN, C_OUT), BF16),
            pltpu.VMEM((9, P_OWN, C_OUT), BF16),
            pltpu.VMEM((P_OWN, C_OUT), BF16),
            pltpu.VMEM((9, P_OWN, C_OUT), BF16),
            pltpu.VMEM((2, T, LX), BF16),
            pltpu.VMEM((2, T, LX), BF16),
            pltpu.VMEM((total, 128), BF16),
            pltpu.VMEM((n_a, shard, 128), BF16),
            pltpu.VMEM((n_b, shard, 128), BF16),
            pltpu.VMEM((total, 128), BF16),
            dma((9,)),
            dma((9,)),
            dma((9,)),
            dma((9,)),
            dma((9,)),
            dma((9,)),
            dma((2,)),
            dma((2,)),
            dma((2,)),
            dma((2,)),
            dma((n_a,)),
            dma((n_a,)),
            dma((n_b,)),
            dma((n_b,)),
            dma((n_a,)),
            dma((n_a,)),
        ],
        compiler_params=pltpu.CompilerParams(
            collective_id=0, has_side_effects=True, vmem_limit_bytes=40 * 1024 * 1024
        ),
    )(*args)


def solution(mesh):
    in_specs = (
        P("row", "col", None),
        P(),
        P(),
        P(),
        P("row", "col"),
        P("row", "col", None),
        P("row", "col", None),
        P("row", "col", None),
    )
    out_specs = (P("row", "col", None), P(), P(), P())
    return jax.shard_map(
        functools.partial(per_device, mesh.shape["row"], mesh.shape["col"]),
        mesh=mesh,
        in_specs=in_specs,
        out_specs=out_specs,
        check_vma=False,
    )
```

```python
import functools

import jax
import jax.numpy as jnp
from jax import lax
from jax.experimental import pallas as pl
from jax.experimental.pallas import tpu as pltpu
from jax.sharding import PartitionSpec as P

DATES = 12
C_IN = 64
C_OUT = 128
GROUPS = 16
CLASSES = 20
P_OWN = 32
S_STR = 32
CPG = 8
EPSILON = 1e-05
PRECISE = lax.Precision.HIGHEST
MESH = pl.DeviceIdType.MESH
F32 = jnp.float32
BF16 = jnp.bfloat16

VMEM_GRANT = 63 * 1024 * 1024
T = 16
PIX = T * T
PAIRS = DATES // 2
LX = DATES * C_IN
LG = DATES * C_OUT
SLOTS = 9 * P_OWN
CONV_ROWS = 9 * C_IN
SMALL_ROWS = 48
DIRS = [d for d in range(9) if d != 4]


def iota(shape, dim):
    return lax.broadcasted_iota(jnp.int32, shape, dim)


def dot(a, b, dims=((1,), (0,)), precision=None):
    return lax.dot_general(
        a, b, (dims, ((), ())), preferred_element_type=F32, precision=precision
    )


def sigmoid(v):
    return 0.5 * jnp.tanh(0.5 * v) + 0.5


def kernel(
    n_row,
    n_col,
    shard,
    x_hbm,
    cw_hbm,
    tw_hbm,
    kw_hbm,
    slot_hbm,
    sdir_hbm,
    sslot_hbm,
    lab_hbm,
    gx_hbm,
    final_hbm,
    gx_ref,
    final,
    out_sems,
    x_ref,
    cw_ref,
    tw_ref,
    kw_ref,
    slot_ref,
    sdir_ref,
    sslot_ref,
    lab_ref,
    in_sems,
    xf,
    xs,
    xc,
    wf,
    wb,
    b4f,
    b4b,
    onehot,
    onehot_t,
    hid,
    gmix,
    hid_t,
    slope_pre,
    slope_mix,
    gpre,
    zs,
    zacc,
    col_send,
    col_recv,
    cor_send,
    cor_recv,
    sum_send,
    sum_recv,
    pgrad,
    beside,
    z_send,
    z_recv,
    part,
    rs_recv,
    bx_recv,
    px_ss,
    px_rs,
    ps_ss,
    ps_rs,
    pg_ss,
    pg_rs,
    gh_ss,
    gh_rs,
    zc_ss,
    zc_rs,
    rs_ss,
    rs_rs,
    bx_ss,
    bx_rs,
    ag_ss,
    ag_rs,
):
    row = lax.axis_index("row")
    col = lax.axis_index("col")
    n_a = 2 * n_col
    n_b = n_row // 2
    base = lax.div(row, 2)
    a_row = lax.rem(row, 2)
    a_me = a_row * n_col + col

    def a_dev(k):
        q = lax.rem(a_me + k, n_a)
        return q, (base * 2 + lax.div(q, n_col), lax.rem(q, n_col))

    def b_dev(k):
        return (lax.rem(base + k, n_b) * 2 + a_row, col)

    def neighbour(d):
        r = row + (d // 3 - 1)
        c = col + (d % 3 - 1)
        there = (r >= 0) & (r < n_row) & (c >= 0) & (c < n_col)
        return there, (r, c)

    fetches = [
        pltpu.make_async_copy(src, dst, in_sems.at[i])
        for i, (src, dst) in enumerate(
            (
                (x_hbm, x_ref),
                (cw_hbm, cw_ref),
                (tw_hbm, tw_ref),
                (kw_hbm, kw_ref),
                (slot_hbm, slot_ref),
                (sdir_hbm, sdir_ref),
                (sslot_hbm, sslot_ref),
                (lab_hbm, lab_ref),
            )
        )
    ]
    for fetch in fetches:
        fetch.start()

    xc[1, 0] = jnp.zeros((T, LX), BF16)
    xc[1, T + 1] = jnp.zeros((T, LX), BF16)
    gpre[0] = jnp.zeros((T, LG), BF16)
    gpre[T + 1] = jnp.zeros((T, LG), BF16)
    col_recv[...] = jnp.zeros(col_recv.shape, BF16)
    cor_recv[...] = jnp.zeros(cor_recv.shape, BF16)
    sum_recv[...] = jnp.zeros(sum_recv.shape, BF16)
    beside[...] = jnp.zeros(beside.shape, BF16)
    z_recv[...] = jnp.zeros(z_recv.shape, BF16)

    barrier = pltpu.get_barrier_semaphore()
    expected = n_a - 1 + n_b - 1
    for d in DIRS:
        there, dev = neighbour(d)
        expected = expected + there.astype(jnp.int32)

        @pl.when(there)
        def _():
            pl.semaphore_signal(barrier, inc=1, device_id=dev, device_id_type=MESH)

    for k in range(1, n_a):
        pl.semaphore_signal(barrier, inc=1, device_id=a_dev(k)[1], device_id_type=MESH)
    for k in range(1, n_b):
        pl.semaphore_signal(barrier, inc=1, device_id=b_dev(k), device_id_type=MESH)

    fetches[0].wait()
    x_own = x_ref[...].astype(F32).reshape(PIX, LX)
    left, right = [], []
    for p in range(PAIRS):
        xf[p] = x_own[:, p * 128 : (p + 1) * 128]
        left.append(xf[p, pl.ds(0, T, stride=T), :])
        right.append(xf[p, pl.ds(T - 1, T, stride=T), :])
        col_send[0, :, p * 128 : (p + 1) * 128] = left[p].astype(BF16)
        col_send[1, :, p * 128 : (p + 1) * 128] = right[p].astype(BF16)
    which = iota((T, 128), 0)
    for corner, source, at in ((0, left, 0), (1, right, 0), (2, left, T - 1), (3, right, T - 1)):
        block = jnp.zeros((T, 128), F32)
        for p in range(PAIRS):
            piece = source[p][at : at + 1, :]
            block = jnp.where(which == p, jnp.broadcast_to(piece, (T, 128)), block)
        cor_send[corner] = block.astype(BF16)

    pl.semaphore_wait(barrier, expected)

    corner_of = {0: 0, 2: 1, 6: 2, 8: 3}

    def pixel_copy(d, dev):
        o = 8 - d
        if d in corner_of:
            src, dst = cor_send.at[corner_of[d]], cor_recv.at[corner_of[o]]
        elif d == 1:
            src, dst = x_ref.at[0], xc.at[1, T + 1]
        elif d == 7:
            src, dst = x_ref.at[T - 1], xc.at[1, 0]
        elif d == 3:
            src, dst = col_send.at[0], col_recv.at[1]
        else:
            src, dst = col_send.at[1], col_recv.at[0]
        return pltpu.make_async_remote_copy(
            src_ref=src,
            dst_ref=dst,
            send_sem=px_ss.at[d],
            recv_sem=px_rs.at[o],
            device_id=dev,
            device_id_type=MESH,
        )

    def sums_copy(d, dev):
        return pltpu.make_async_remote_copy(
            src_ref=sum_send.at[d],
            dst_ref=sum_recv.at[8 - d],
            send_sem=ps_ss.at[d],
            recv_sem=ps_rs.at[8 - d],
            device_id=dev,
            device_id_type=MESH,
        )

    def grad_copy(d, dev):
        return pltpu.make_async_remote_copy(
            src_ref=pgrad,
            dst_ref=beside.at[8 - d],
            send_sem=pg_ss.at[d],
            recv_sem=pg_rs.at[8 - d],
            device_id=dev,
            device_id_type=MESH,
        )

    def row_copy(d, dev):
        k = 0 if d == 1 else 1
        return pltpu.make_async_remote_copy(
            src_ref=gpre.at[1 if d == 1 else T],
            dst_ref=gpre.at[T + 1 if d == 1 else 0],
            send_sem=gh_ss.at[k],
            recv_sem=gh_rs.at[1 - k],
            device_id=dev,
            device_id_type=MESH,
        )

    def col_copy(d, dev):
        k = 0 if d == 3 else 1
        return pltpu.make_async_remote_copy(
            src_ref=z_send.at[k],
            dst_ref=z_recv.at[1 - k],
            send_sem=zc_ss.at[k],
            recv_sem=zc_rs.at[1 - k],
            device_id=dev,
            device_id_type=MESH,
        )

    def start_all(make, dirs):
        for d in dirs:
            there, dev = neighbour(d)

            @pl.when(there)
            def _():
                make(d, dev).start()

    def wait_recv_all(make, dirs):
        for d in dirs:
            there, dev = neighbour(d)

            @pl.when(there)
            def _():
                make(8 - d, dev).wait_recv()

    def wait_send_all(make, dirs):
        for d in dirs:
            there, dev = neighbour(d)

            @pl.when(there)
            def _():
                make(d, dev).wait_send()

    start_all(pixel_copy, DIRS)

    for fetch in fetches[1:]:
        fetch.wait()
    xc[1, 1 : T + 1] = x_ref[...]
    wf[...] = jnp.zeros(wf.shape, BF16)
    for r in range(3):
        for c in range(3):
            t = r * 3 + c
            w = cw_ref[r, c]
            wf[t * 128 : t * 128 + 64, 0:128] = w
            wf[t * 128 + 64 : t * 128 + 128, 128:256] = w
    for r in range(3):
        for slot_at, c in ((0, 0), (1, 2), (2, 1)):
            t = r * 3 + c
            block = wf[t * 128 : (t + 1) * 128, :].astype(F32)
            wb[r * 256 : (r + 1) * 256, slot_at * 128 : (slot_at + 1) * 128] = block.T.astype(BF16)
    same_group = lax.div(iota((128, 128), 0), CPG) == lax.div(iota((128, 128), 1), CPG)
    width = 3 * CPG * CPG
    by_group = (lax.div(iota((128, GROUPS), 0), CPG) == iota((128, GROUPS), 1)).astype(BF16)
    compact = tw_ref[...].astype(F32).reshape(width, GROUPS).astype(BF16)
    spread_rows = dot(by_group, compact, ((1,), (1,)))
    entry = iota((128, width), 1)
    in_chan = lax.rem(iota((128, width), 0), CPG)
    fold_out = (
        lax.rem(iota((width, 128), 0), CPG) == lax.rem(iota((width, 128), 1), CPG)
    ).astype(BF16)
    dense, dense_t = [], []
    for tap in range(3):
        rows = jnp.where(lax.div(entry, CPG) == tap * CPG + in_chan, spread_rows, 0.0)
        d_tap = jnp.where(same_group, dot(rows.astype(BF16), fold_out), 0.0)
        dense.append(d_tap.astype(BF16))
        dense_t.append(d_tap.T.astype(BF16))
    nothing = jnp.zeros((128, 128), BF16)
    for ref, (one, two, three) in ((b4f, dense), (b4b, dense_t[::-1])):
        for i, (lo, hi) in enumerate(((one, nothing), (two, one), (three, two), (nothing, three))):
            ref[i * 128 : (i + 1) * 128, 0:128] = lo
            ref[i * 128 : (i + 1) * 128, 128:256] = hi
    zero_side = jnp.zeros((PIX, 128), BF16)
    hid[:, 0:128] = zero_side
    hid[:, 128 + LG : 256 + LG] = zero_side
    gmix[:, 0:128] = zero_side
    gmix[:, 128 + LG : 256 + LG] = zero_side

    pick_row = (lax.div(iota((PIX, T), 0), T) == iota((PIX, T), 1)).astype(BF16)
    by_row = dot(pick_row, slot_ref[...].astype(F32).astype(BF16))
    at_col = lax.rem(iota((PIX, T), 0), T) == iota((PIX, T), 1)
    slot_of = jnp.sum(jnp.where(at_col, by_row, 0.0), axis=1, keepdims=True).astype(jnp.int32)
    in_own = (slot_of == iota((PIX, P_OWN), 1)).astype(BF16)
    in_str = (slot_of - P_OWN == iota((PIX, S_STR), 1)).astype(BF16)
    target = sdir_ref[0] * P_OWN + sslot_ref[0]
    sel_own = (iota((SLOTS, P_OWN), 0) == iota((SLOTS, P_OWN), 1) + 4 * P_OWN).astype(BF16)
    sel_str = (iota((SLOTS, S_STR), 0) == target).astype(BF16)
    onehot[...] = (
        dot(sel_own, in_own, ((1,), (1,))) + dot(sel_str, in_str, ((1,), (1,)))
    ).astype(BF16)
    onehot_t[...] = (
        dot(in_own, sel_own, ((1,), (1,))) + dot(in_str, sel_str, ((1,), (1,)))
    ).astype(BF16)

    for p in range(PAIRS):
        lanes = x_own[:, p * 128 : (p + 1) * 128]
        xs[0, p, T : T + PIX] = pltpu.roll(lanes, 1, 0)
        xs[1, p, T : T + PIX] = pltpu.roll(lanes, PIX - 1, 0)
    wait_recv_all(pixel_copy, DIRS)
    for halo in (0, T + 1):
        line = xc[1, halo].astype(F32)
        for p in range(PAIRS):
            lanes = line[:, p * 128 : (p + 1) * 128]
            xs[0, p, halo * T : (halo + 1) * T] = pltpu.roll(lanes, 1, 0)
            xs[1, p, halo * T : (halo + 1) * T] = pltpu.roll(lanes, T - 1, 0)
    for side, at in ((0, 0), (1, T - 1)):
        arrived = col_recv[side].astype(F32)
        top = cor_recv[side].astype(F32)
        bottom = cor_recv[2 + side].astype(F32)
        last = (T + 1) * T
        for p in range(PAIRS):
            lanes = slice(p * 128, (p + 1) * 128)
            xs[side, p, pl.ds(T + at, T, stride=T), :] = arrived[:, lanes]
            xs[side, p, at : at + 1, :] = top[p : p + 1, :]
            xs[side, p, last + at : last + at + 1, :] = bottom[p : p + 1, :]
            xc[2 * side, :, :, lanes] = xs[side, p].astype(BF16).reshape(T + 2, T, 128)

    def taps(p):
        return jnp.concatenate(
            [
                xc[c, r : r + T, :, p * 128 : (p + 1) * 128].reshape(PIX, 128)
                for r in range(3)
                for c in range(3)
            ],
            axis=1,
        )

    for p in range(PAIRS):
        pre = dot(taps(p), wf[...])
        sig = sigmoid(pre)
        act = pre * sig
        slope_pre[:, p * 256 : (p + 1) * 256] = sig + act * (1.0 - sig)
        hid[:, 128 + p * 256 : 128 + (p + 1) * 256] = act.astype(BF16)
    total = jnp.zeros((PIX, 256), F32)
    for p in range(PAIRS):
        mixed = dot(hid[:, p * 256 : p * 256 + 512], b4f[...])
        sig = sigmoid(mixed)
        act = mixed * sig
        slope_mix[:, p * 256 : (p + 1) * 256] = (sig + act * (1.0 - sig)) * (1.0 / DATES)
        total = total + act
    embedded = ((total[:, 0:128] + total[:, 128:256]) * (1.0 / DATES)).astype(BF16)
    outgoing = dot(onehot[...], embedded)
    for d in DIRS:
        sum_send[d] = outgoing[d * P_OWN : (d + 1) * P_OWN].astype(BF16)
    start_all(sums_copy, DIRS)
    sums = outgoing[4 * P_OWN : 5 * P_OWN]
    for p in range(PAIRS):
        hid_t[p * 256 : (p + 1) * 256, :] = hid[:, 128 + p * 256 : 128 + (p + 1) * 256].T
    wait_recv_all(sums_copy, DIRS)
    for d in DIRS:
        sums = sums + sum_recv[d].astype(F32)

    centered = sums - jnp.mean(sums, axis=-1, keepdims=True)
    inverse = lax.rsqrt(jnp.mean(centered * centered, axis=-1, keepdims=True) + EPSILON)
    normed = centered * inverse
    rounded = normed.astype(BF16)
    kw = kw_ref[...]
    logits = dot(rounded, kw, ((1,), (1,)))
    exps = jnp.exp(logits)
    prob = exps / jnp.sum(exps, axis=-1, keepdims=True)
    lab = lab_ref[0]
    lab_col = jnp.sum(
        jnp.where(iota((P_OWN, P_OWN), 0) == iota((P_OWN, P_OWN), 1), lab.astype(F32), 0.0),
        axis=1,
        keepdims=True,
    ).astype(jnp.int32)
    hot = (lab_col == iota((P_OWN, CLASSES), 1)).astype(F32)
    g_logits = (prob - hot) * (1.0 / (P_OWN * n_row * n_col))
    g_normed = dot(g_logits, kw.astype(F32), ((1,), (0,)), PRECISE)
    g_parcel = inverse * (
        g_normed
        - jnp.mean(g_normed, axis=-1, keepdims=True)
        - normed * jnp.mean(g_normed * normed, axis=-1, keepdims=True)
    )
    g_parcel = g_parcel.astype(BF16)
    pgrad[...] = g_parcel
    start_all(grad_copy, DIRS)
    beside[4] = g_parcel
    class_term = dot(g_logits, rounded.astype(F32), ((0,), (0,)), PRECISE)
    wait_recv_all(grad_copy, DIRS)

    pixel_grad = dot(onehot_t[...], beside[...].reshape(SLOTS, C_OUT))
    pixel_grad = jnp.concatenate([pixel_grad, pixel_grad], axis=1)
    for p in range(PAIRS):
        gmix[:, 128 + p * 256 : 128 + (p + 1) * 256] = (
            pixel_grad * slope_mix[:, p * 256 : (p + 1) * 256]
        ).astype(BF16)
    for p in range(PAIRS):
        g_hid = dot(gmix[:, p * 256 : p * 256 + 512], b4b[...])
        g_pre = (g_hid * slope_pre[:, p * 256 : (p + 1) * 256]).astype(BF16)
        gpre[1 : T + 1, :, p * 256 : (p + 1) * 256] = g_pre.reshape(T, T, 256)
    start_all(row_copy, (1, 7))

    conv_t = None
    for p in range(PAIRS):
        g_pair = gpre[1 : T + 1, :, p * 256 : (p + 1) * 256].reshape(PIX, 256)
        term = dot(g_pair, taps(p), ((0,), (0,)))
        conv_t = term if conv_t is None else conv_t + term
    low_half = iota((128, 128), 1) < C_IN
    for t in range(9):
        both = jnp.where(
            low_half,
            conv_t[0:128, t * 128 : (t + 1) * 128],
            conv_t[128:256, t * 128 : (t + 1) * 128],
        ).T
        part[t * 64 : (t + 1) * 64, :] = (both[0:64] + both[64:128]).astype(BF16)
    even = None
    for p in range(PAIRS):
        term = dot(
            hid_t[p * 256 : (p + 1) * 256, :], gmix[:, 128 + p * 256 : 128 + (p + 1) * 256]
        )
        even = term if even is None else even + term
    odd = None
    for p in range(PAIRS - 1):
        term = dot(
            hid_t[p * 256 + 128 : p * 256 + 384, :],
            gmix[:, 256 + p * 256 : 512 + p * 256],
        )
        odd = term if odd is None else odd + term
    time_taps = (
        even[0:128, 128:256] + odd[0:128, 128:256],
        even[0:128, 0:128] + even[128:256, 128:256],
        even[128:256, 0:128] + odd[128:256, 0:128],
    )
    small = [
        jnp.sum(jnp.where(same_group, tap, 0.0).reshape(GROUPS, CPG, 128), axis=0)
        for tap in time_taps
    ]
    small.append(class_term)
    small.append(jnp.zeros((SMALL_ROWS - 3 * CPG - CLASSES, 128), F32))
    part[CONV_ROWS : CONV_ROWS + SMALL_ROWS, :] = jnp.concatenate(small, axis=0).astype(BF16)

    def shard_at(q):
        return pl.ds(pl.multiple_of(q * shard, 16), shard)

    def rs_copy(k):
        q, dev = a_dev(k)
        return pltpu.make_async_remote_copy(
            src_ref=part.at[shard_at(q)],
            dst_ref=rs_recv.at[k],
            send_sem=rs_ss.at[k],
            recv_sem=rs_rs.at[k],
            device_id=dev,
            device_id_type=MESH,
        )

    def bx_copy(k):
        return pltpu.make_async_remote_copy(
            src_ref=bx_recv.at[base],
            dst_ref=bx_recv.at[base],
            send_sem=bx_ss.at[k],
            recv_sem=bx_rs.at[k],
            device_id=b_dev(k),
            device_id_type=MESH,
        )

    def ag_copy(k):
        return pltpu.make_async_remote_copy(
            src_ref=final.at[shard_at(a_me)],
            dst_ref=final.at[shard_at(a_me)],
            send_sem=ag_ss.at[k],
            recv_sem=ag_rs.at[k],
            device_id=a_dev(k)[1],
            device_id_type=MESH,
        )

    for k in range(1, n_a):
        rs_copy(k).start()

    wait_recv_all(row_copy, (1, 7))
    j_at = lax.rem(iota((PIX, 128), 0), T)
    for p in range(PAIRS):
        g_rows = jnp.concatenate(
            [
                gpre[2 - r : 2 - r + T, :, p * 256 : (p + 1) * 256].reshape(PIX, 256)
                for r in range(3)
            ],
            axis=1,
        )
        z = dot(g_rows, wb[...])
        zs[0] = z[:, 0:128]
        zs[1] = z[:, 128:256]
        z_send[0, :, p * 128 : (p + 1) * 128] = zs[0, pl.ds(0, T, stride=T), :].astype(BF16)
        z_send[1, :, p * 128 : (p + 1) * 128] = zs[1, pl.ds(T - 1, T, stride=T), :].astype(BF16)
        from_right = jnp.where(j_at == T - 1, 0.0, pltpu.roll(z[:, 0:128], PIX - 1, 0))
        from_left = jnp.where(j_at == 0, 0.0, pltpu.roll(z[:, 128:256], 1, 0))
        zacc[p] = z[:, 256:384] + from_right + from_left
    start_all(col_copy, (3, 5))

    mine = part[shard_at(a_me)].astype(F32)
    for k in range(1, n_a):
        rs_copy(k).wait_recv()
    for k in range(1, n_a):
        mine = mine + rs_recv[k].astype(F32)
    bx_recv[base] = mine.astype(BF16)
    for k in range(1, n_b):
        bx_copy(k).start()

    wait_recv_all(col_copy, (3, 5))
    for p in range(PAIRS):
        lanes = slice(p * 128, (p + 1) * 128)
        at_left = zacc[p, pl.ds(0, T, stride=T), :] + z_recv[0, :, lanes].astype(F32)
        zacc[p, pl.ds(0, T, stride=T), :] = at_left
        at_right = zacc[p, pl.ds(T - 1, T, stride=T), :] + z_recv[1, :, lanes].astype(F32)
        zacc[p, pl.ds(T - 1, T, stride=T), :] = at_right
        gx_ref[:, :, lanes] = zacc[p].astype(BF16).reshape(T, T, 128)

    gx_store = pltpu.make_async_copy(gx_ref, gx_hbm, out_sems.at[0])
    gx_store.start()
    for k in range(1, n_b):
        pltpu.make_async_remote_copy(
            src_ref=bx_recv.at[base],
            dst_ref=bx_recv.at[lax.rem(base + n_b - k, n_b)],
            send_sem=bx_ss.at[k],
            recv_sem=bx_rs.at[k],
            device_id=b_dev(k),
            device_id_type=MESH,
        ).wait_recv()
    whole = bx_recv[0].astype(F32)
    for g in range(1, n_b):
        whole = whole + bx_recv[g].astype(F32)
    final[shard_at(a_me)] = whole.astype(BF16)
    for k in range(1, n_a):
        ag_copy(k).start()
    wait_send_all(pixel_copy, DIRS)
    wait_send_all(sums_copy, DIRS)
    wait_send_all(grad_copy, DIRS)
    wait_send_all(row_copy, (1, 7))
    wait_send_all(col_copy, (3, 5))
    for k in range(1, n_a):
        rs_copy(k).wait_send()
    for k in range(1, n_b):
        bx_copy(k).wait_send()
    for k in range(1, n_a):
        q = lax.rem(a_me + n_a - k, n_a)
        pltpu.make_async_remote_copy(
            src_ref=final.at[shard_at(a_me)],
            dst_ref=final.at[shard_at(q)],
            send_sem=ag_ss.at[k],
            recv_sem=ag_rs.at[k],
            device_id=a_dev(k)[1],
            device_id_type=MESH,
        ).wait_recv()
    final_store = pltpu.make_async_copy(final, final_hbm, out_sems.at[1])
    final_store.start()
    for k in range(1, n_a):
        ag_copy(k).wait_send()
    gx_store.wait()
    final_store.wait()


def finish(gx_in, final, gx_out, gcw_ref, gtw_ref, gkw_ref, sem):
    copy = pltpu.make_async_copy(gx_in, gx_out, sem)
    copy.start()
    for t in range(9):
        gcw_ref[t // 3, t % 3] = final[t * 64 : (t + 1) * 64, :].astype(F32)
    width = 3 * CPG * CPG
    small = final[CONV_ROWS : CONV_ROWS + SMALL_ROWS, :]
    repeat = (lax.div(iota((width, SMALL_ROWS), 0), CPG) == iota((width, SMALL_ROWS), 1)).astype(
        BF16
    )
    rows = dot(repeat, small)
    own_out = lax.rem(iota((width, 128), 0), CPG) == lax.rem(iota((width, 128), 1), CPG)
    fold = (lax.div(iota((128, GROUPS), 0), CPG) == iota((128, GROUPS), 1)).astype(BF16)
    rows = jnp.where(own_out, rows, 0.0).astype(BF16)
    gtw_ref[...] = dot(rows, fold).reshape(3, CPG, CPG, GROUPS)
    gkw_ref[...] = small[3 * CPG : 3 * CPG + CLASSES].astype(F32)
    copy.wait()


def per_device(n_row, n_col, pixels, conv_weight, time_weight, class_weight, *rest):
    args = (pixels, conv_weight, time_weight.transpose(0, 2, 3, 1), class_weight.T, *rest)
    n_a = 2 * n_col
    n_b = n_row // 2
    rows = CONV_ROWS + SMALL_ROWS
    shard = -(-rows // (16 * n_a)) * 16
    total = shard * n_a
    vmem = pl.BlockSpec(memory_space=pltpu.VMEM)
    dma = pltpu.SemaphoreType.DMA
    anywhere = pl.BlockSpec(memory_space=pl.ANY)
    gx, final = pl.pallas_call(
        functools.partial(kernel, n_row, n_col, shard),
        out_shape=(
            jax.ShapeDtypeStruct((T, T, LX), BF16),
            jax.ShapeDtypeStruct((total, 128), BF16),
        ),
        in_specs=[anywhere] * 8,
        out_specs=(anywhere,) * 2,
        scratch_shapes=[
            pltpu.VMEM((T, T, LX), BF16),
            pltpu.VMEM((total, 128), BF16),
            dma((2,)),
            *[pltpu.VMEM(arg.shape, arg.dtype) for arg in args],
            dma((8,)),
            pltpu.VMEM((PAIRS, PIX, 128), F32),
            pltpu.VMEM((2, PAIRS, PIX + 2 * T, 128), F32),
            pltpu.VMEM((3, T + 2, T, LX), BF16),
            pltpu.VMEM((9 * 128, 256), BF16),
            pltpu.VMEM((3 * 256, 3 * 128), BF16),
            pltpu.VMEM((512, 256), BF16),
            pltpu.VMEM((512, 256), BF16),
            pltpu.VMEM((SLOTS, PIX), BF16),
            pltpu.VMEM((PIX, SLOTS), BF16),
            pltpu.VMEM((PIX, LG + 256), BF16),
            pltpu.VMEM((PIX, LG + 256), BF16),
            pltpu.VMEM((LG, PIX), BF16),
            pltpu.VMEM((PIX, LG), F32),
            pltpu.VMEM((PIX, LG), F32),
            pltpu.VMEM((T + 2, T, LG), BF16),
            pltpu.VMEM((2, PIX, 128), F32),
            pltpu.VMEM((PAIRS, PIX, 128), F32),
            pltpu.VMEM((2, T, LX), BF16),
            pltpu.VMEM((2, T, LX), BF16),
            pltpu.VMEM((4, T, 128), BF16),
            pltpu.VMEM((4, T, 128), BF16),
            pltpu.VMEM((9, P_OWN, C_OUT), BF16),
            pltpu.VMEM((9, P_OWN, C_OUT), BF16),
            pltpu.VMEM((P_OWN, C_OUT), BF16),
            pltpu.VMEM((9, P_OWN, C_OUT), BF16),
            pltpu.VMEM((2, T, LX), BF16),
            pltpu.VMEM((2, T, LX), BF16),
            pltpu.VMEM((total, 128), BF16),
            pltpu.VMEM((n_a, shard, 128), BF16),
            pltpu.VMEM((n_b, shard, 128), BF16),
            dma((9,)),
            dma((9,)),
            dma((9,)),
            dma((9,)),
            dma((9,)),
            dma((9,)),
            dma((2,)),
            dma((2,)),
            dma((2,)),
            dma((2,)),
            dma((n_a,)),
            dma((n_a,)),
            dma((n_b,)),
            dma((n_b,)),
            dma((n_a,)),
            dma((n_a,)),
        ],
        compiler_params=pltpu.CompilerParams(
            collective_id=0, has_side_effects=True, vmem_limit_bytes=VMEM_GRANT
        ),
    )(*args)
    gx, conv_grad, time_grad, class_grad = pl.pallas_call(
        finish,
        out_shape=(
            jax.ShapeDtypeStruct((T, T, LX), BF16),
            jax.ShapeDtypeStruct((3, 3, C_IN, C_OUT), F32),
            jax.ShapeDtypeStruct((3, CPG, CPG, GROUPS), F32),
            jax.ShapeDtypeStruct((CLASSES, C_OUT), F32),
        ),
        in_specs=[anywhere, vmem],
        out_specs=(anywhere, vmem, vmem, vmem),
        scratch_shapes=[dma],
        compiler_params=pltpu.CompilerParams(vmem_limit_bytes=VMEM_GRANT),
    )(gx, final)
    return gx, conv_grad, time_grad.transpose(0, 3, 1, 2), class_grad.T


def solution(mesh):
    in_specs = (
        P("row", "col", None),
        P(),
        P(),
        P(),
        P("row", "col"),
        P("row", "col", None),
        P("row", "col", None),
        P("row", "col", None),
    )
    out_specs = (P("row", "col", None), P(), P(), P())
    return jax.shard_map(
        functools.partial(per_device, mesh.shape["row"], mesh.shape["col"]),
        mesh=mesh,
        in_specs=in_specs,
        out_specs=out_specs,
        check_vma=False,
    )
```

```python
import functools

import jax
import jax.numpy as jnp
from jax import lax
from jax.experimental import pallas as pl
from jax.experimental.pallas import tpu as pltpu
from jax.sharding import PartitionSpec as P

DATES = 12
C_IN = 64
C_OUT = 128
GROUPS = 16
CLASSES = 20
P_OWN = 32
S_STR = 32
CPG = 8
EPSILON = 1e-05
PRECISE = lax.Precision.HIGHEST
MESH = pl.DeviceIdType.MESH
F32 = jnp.float32
BF16 = jnp.bfloat16

VMEM_GRANT = 63 * 1024 * 1024
CHUNKS = 4
T = 16
PIX = T * T
PAIRS = DATES // 2
LX = DATES * C_IN
LG = DATES * C_OUT
SLOTS = 9 * P_OWN
CONV_ROWS = 9 * C_IN
SMALL_ROWS = 48
DIRS = [d for d in range(9) if d != 4]


def iota(shape, dim):
    return lax.broadcasted_iota(jnp.int32, shape, dim)


def dot(a, b, dims=((1,), (0,)), precision=None):
    return lax.dot_general(
        a, b, (dims, ((), ())), preferred_element_type=F32, precision=precision
    )


def sigmoid(v):
    return 0.5 * jnp.tanh(0.5 * v) + 0.5


def kernel(
    n_row,
    n_col,
    shard,
    x_hbm,
    cw_hbm,
    tw_hbm,
    kw_hbm,
    slot_hbm,
    sdir_hbm,
    sslot_hbm,
    lab_hbm,
    gx_hbm,
    final_hbm,
    gx_ref,
    final,
    out_sems,
    x_ref,
    cw_ref,
    tw_ref,
    kw_ref,
    slot_ref,
    sdir_ref,
    sslot_ref,
    lab_ref,
    in_sems,
    xf,
    xs,
    xc,
    wf,
    wb,
    b4f,
    b4b,
    onehot,
    onehot_t,
    hid,
    gmix,
    hid_t,
    slope_pre,
    slope_mix,
    gpre,
    zs,
    zacc,
    col_send,
    col_recv,
    cor_send,
    cor_recv,
    sum_send,
    sum_recv,
    pgrad,
    beside,
    z_send,
    z_recv,
    part,
    rs_recv,
    bx_recv,
    px_ss,
    px_rs,
    ps_ss,
    ps_rs,
    pg_ss,
    pg_rs,
    gh_ss,
    gh_rs,
    zc_ss,
    zc_rs,
    rs_ss,
    rs_rs,
    bx_ss,
    bx_rs,
    ag_ss,
    ag_rs,
):
    row = lax.axis_index("row")
    col = lax.axis_index("col")
    n_a = 2 * n_col
    n_b = n_row // 2
    base = lax.div(row, 2)
    a_row = lax.rem(row, 2)
    a_me = a_row * n_col + col

    def a_dev(k):
        q = lax.rem(a_me + k, n_a)
        return q, (base * 2 + lax.div(q, n_col), lax.rem(q, n_col))

    def b_dev(k):
        return (lax.rem(base + k, n_b) * 2 + a_row, col)

    def neighbour(d):
        r = row + (d // 3 - 1)
        c = col + (d % 3 - 1)
        there = (r >= 0) & (r < n_row) & (c >= 0) & (c < n_col)
        return there, (r, c)

    fetches = [
        pltpu.make_async_copy(src, dst, in_sems.at[i])
        for i, (src, dst) in enumerate(
            (
                (x_hbm, x_ref),
                (cw_hbm, cw_ref),
                (tw_hbm, tw_ref),
                (kw_hbm, kw_ref),
                (slot_hbm, slot_ref),
                (sdir_hbm, sdir_ref),
                (sslot_hbm, sslot_ref),
                (lab_hbm, lab_ref),
            )
        )
    ]
    for fetch in fetches:
        fetch.start()

    xc[1, 0] = jnp.zeros((T, LX), BF16)
    xc[1, T + 1] = jnp.zeros((T, LX), BF16)
    gpre[0] = jnp.zeros((T, LG), BF16)
    gpre[T + 1] = jnp.zeros((T, LG), BF16)
    col_recv[...] = jnp.zeros(col_recv.shape, BF16)
    cor_recv[...] = jnp.zeros(cor_recv.shape, BF16)
    sum_recv[...] = jnp.zeros(sum_recv.shape, BF16)
    beside[...] = jnp.zeros(beside.shape, BF16)
    z_recv[...] = jnp.zeros(z_recv.shape, BF16)

    barrier = pltpu.get_barrier_semaphore()
    expected = n_a - 1 + n_b - 1
    for d in DIRS:
        there, dev = neighbour(d)
        expected = expected + there.astype(jnp.int32)

        @pl.when(there)
        def _():
            pl.semaphore_signal(barrier, inc=1, device_id=dev, device_id_type=MESH)

    for k in range(1, n_a):
        pl.semaphore_signal(barrier, inc=1, device_id=a_dev(k)[1], device_id_type=MESH)
    for k in range(1, n_b):
        pl.semaphore_signal(barrier, inc=1, device_id=b_dev(k), device_id_type=MESH)

    fetches[0].wait()
    x_own = x_ref[...].astype(F32).reshape(PIX, LX)
    left, right = [], []
    for p in range(PAIRS):
        xf[p] = x_own[:, p * 128 : (p + 1) * 128]
        left.append(xf[p, pl.ds(0, T, stride=T), :])
        right.append(xf[p, pl.ds(T - 1, T, stride=T), :])
        col_send[0, :, p * 128 : (p + 1) * 128] = left[p].astype(BF16)
        col_send[1, :, p * 128 : (p + 1) * 128] = right[p].astype(BF16)
    which = iota((T, 128), 0)
    for corner, source, at in ((0, left, 0), (1, right, 0), (2, left, T - 1), (3, right, T - 1)):
        block = jnp.zeros((T, 128), F32)
        for p in range(PAIRS):
            piece = source[p][at : at + 1, :]
            block = jnp.where(which == p, jnp.broadcast_to(piece, (T, 128)), block)
        cor_send[corner] = block.astype(BF16)

    pl.semaphore_wait(barrier, expected)

    corner_of = {0: 0, 2: 1, 6: 2, 8: 3}

    def pixel_copy(d, dev):
        o = 8 - d
        if d in corner_of:
            src, dst = cor_send.at[corner_of[d]], cor_recv.at[corner_of[o]]
        elif d == 1:
            src, dst = x_ref.at[0], xc.at[1, T + 1]
        elif d == 7:
            src, dst = x_ref.at[T - 1], xc.at[1, 0]
        elif d == 3:
            src, dst = col_send.at[0], col_recv.at[1]
        else:
            src, dst = col_send.at[1], col_recv.at[0]
        return pltpu.make_async_remote_copy(
            src_ref=src,
            dst_ref=dst,
            send_sem=px_ss.at[d],
            recv_sem=px_rs.at[o],
            device_id=dev,
            device_id_type=MESH,
        )

    def sums_copy(d, dev):
        return pltpu.make_async_remote_copy(
            src_ref=sum_send.at[d],
            dst_ref=sum_recv.at[8 - d],
            send_sem=ps_ss.at[d],
            recv_sem=ps_rs.at[8 - d],
            device_id=dev,
            device_id_type=MESH,
        )

    def grad_copy(d, dev):
        return pltpu.make_async_remote_copy(
            src_ref=pgrad,
            dst_ref=beside.at[8 - d],
            send_sem=pg_ss.at[d],
            recv_sem=pg_rs.at[8 - d],
            device_id=dev,
            device_id_type=MESH,
        )

    def row_copy(d, dev):
        k = 0 if d == 1 else 1
        return pltpu.make_async_remote_copy(
            src_ref=gpre.at[1 if d == 1 else T],
            dst_ref=gpre.at[T + 1 if d == 1 else 0],
            send_sem=gh_ss.at[k],
            recv_sem=gh_rs.at[1 - k],
            device_id=dev,
            device_id_type=MESH,
        )

    def col_copy(d, dev):
        k = 0 if d == 3 else 1
        return pltpu.make_async_remote_copy(
            src_ref=z_send.at[k],
            dst_ref=z_recv.at[1 - k],
            send_sem=zc_ss.at[k],
            recv_sem=zc_rs.at[1 - k],
            device_id=dev,
            device_id_type=MESH,
        )

    def start_all(make, dirs):
        for d in dirs:
            there, dev = neighbour(d)

            @pl.when(there)
            def _():
                make(d, dev).start()

    def wait_recv_all(make, dirs):
        for d in dirs:
            there, dev = neighbour(d)

            @pl.when(there)
            def _():
                make(8 - d, dev).wait_recv()

    def wait_send_all(make, dirs):
        for d in dirs:
            there, dev = neighbour(d)

            @pl.when(there)
            def _():
                make(d, dev).wait_send()

    start_all(pixel_copy, DIRS)

    for fetch in fetches[1:]:
        fetch.wait()
    xc[1, 1 : T + 1] = x_ref[...]
    wf[...] = jnp.zeros(wf.shape, BF16)
    for r in range(3):
        for c in range(3):
            t = r * 3 + c
            w = cw_ref[r, c]
            wf[t * 128 : t * 128 + 64, 0:128] = w
            wf[t * 128 + 64 : t * 128 + 128, 128:256] = w
    for r in range(3):
        for slot_at, c in ((0, 0), (1, 2), (2, 1)):
            t = r * 3 + c
            block = wf[t * 128 : (t + 1) * 128, :].astype(F32)
            wb[r * 256 : (r + 1) * 256, slot_at * 128 : (slot_at + 1) * 128] = block.T.astype(BF16)
    same_group = lax.div(iota((128, 128), 0), CPG) == lax.div(iota((128, 128), 1), CPG)
    width = 3 * CPG * CPG
    by_group = (lax.div(iota((128, GROUPS), 0), CPG) == iota((128, GROUPS), 1)).astype(BF16)
    compact = tw_ref[...].astype(F32).reshape(width, GROUPS).astype(BF16)
    spread_rows = dot(by_group, compact, ((1,), (1,)))
    entry = iota((128, width), 1)
    in_chan = lax.rem(iota((128, width), 0), CPG)
    fold_out = (
        lax.rem(iota((width, 128), 0), CPG) == lax.rem(iota((width, 128), 1), CPG)
    ).astype(BF16)
    dense, dense_t = [], []
    for tap in range(3):
        rows = jnp.where(lax.div(entry, CPG) == tap * CPG + in_chan, spread_rows, 0.0)
        d_tap = jnp.where(same_group, dot(rows.astype(BF16), fold_out), 0.0)
        dense.append(d_tap.astype(BF16))
        dense_t.append(d_tap.T.astype(BF16))
    nothing = jnp.zeros((128, 128), BF16)
    for ref, (one, two, three) in ((b4f, dense), (b4b, dense_t[::-1])):
        for i, (lo, hi) in enumerate(((one, nothing), (two, one), (three, two), (nothing, three))):
            ref[i * 128 : (i + 1) * 128, 0:128] = lo
            ref[i * 128 : (i + 1) * 128, 128:256] = hi
    zero_side = jnp.zeros((PIX, 128), BF16)
    hid[:, 0:128] = zero_side
    hid[:, 128 + LG : 256 + LG] = zero_side
    gmix[:, 0:128] = zero_side
    gmix[:, 128 + LG : 256 + LG] = zero_side

    pick_row = (lax.div(iota((PIX, T), 0), T) == iota((PIX, T), 1)).astype(BF16)
    by_row = dot(pick_row, slot_ref[...].astype(F32).astype(BF16))
    at_col = lax.rem(iota((PIX, T), 0), T) == iota((PIX, T), 1)
    slot_of = jnp.sum(jnp.where(at_col, by_row, 0.0), axis=1, keepdims=True).astype(jnp.int32)
    in_own = (slot_of == iota((PIX, P_OWN), 1)).astype(BF16)
    in_str = (slot_of - P_OWN == iota((PIX, S_STR), 1)).astype(BF16)
    target = sdir_ref[0] * P_OWN + sslot_ref[0]
    sel_own = (iota((SLOTS, P_OWN), 0) == iota((SLOTS, P_OWN), 1) + 4 * P_OWN).astype(BF16)
    sel_str = (iota((SLOTS, S_STR), 0) == target).astype(BF16)
    onehot[...] = (
        dot(sel_own, in_own, ((1,), (1,))) + dot(sel_str, in_str, ((1,), (1,)))
    ).astype(BF16)
    onehot_t[...] = (
        dot(in_own, sel_own, ((1,), (1,))) + dot(in_str, sel_str, ((1,), (1,)))
    ).astype(BF16)

    for p in range(PAIRS):
        lanes = x_own[:, p * 128 : (p + 1) * 128]
        xs[0, p, T : T + PIX] = pltpu.roll(lanes, 1, 0)
        xs[1, p, T : T + PIX] = pltpu.roll(lanes, PIX - 1, 0)
    wait_recv_all(pixel_copy, DIRS)
    for halo in (0, T + 1):
        line = xc[1, halo].astype(F32)
        for p in range(PAIRS):
            lanes = line[:, p * 128 : (p + 1) * 128]
            xs[0, p, halo * T : (halo + 1) * T] = pltpu.roll(lanes, 1, 0)
            xs[1, p, halo * T : (halo + 1) * T] = pltpu.roll(lanes, T - 1, 0)
    for side, at in ((0, 0), (1, T - 1)):
        arrived = col_recv[side].astype(F32)
        top = cor_recv[side].astype(F32)
        bottom = cor_recv[2 + side].astype(F32)
        last = (T + 1) * T
        for p in range(PAIRS):
            lanes = slice(p * 128, (p + 1) * 128)
            xs[side, p, pl.ds(T + at, T, stride=T), :] = arrived[:, lanes]
            xs[side, p, at : at + 1, :] = top[p : p + 1, :]
            xs[side, p, last + at : last + at + 1, :] = bottom[p : p + 1, :]
            xc[2 * side, :, :, lanes] = xs[side, p].astype(BF16).reshape(T + 2, T, 128)

    def taps(p):
        return jnp.concatenate(
            [
                xc[c, r : r + T, :, p * 128 : (p + 1) * 128].reshape(PIX, 128)
                for r in range(3)
                for c in range(3)
            ],
            axis=1,
        )

    for p in range(PAIRS):
        pre = dot(taps(p), wf[...])
        sig = sigmoid(pre)
        act = pre * sig
        slope_pre[:, p * 256 : (p + 1) * 256] = sig + act * (1.0 - sig)
        hid[:, 128 + p * 256 : 128 + (p + 1) * 256] = act.astype(BF16)
    total = jnp.zeros((PIX, 256), F32)
    for p in range(PAIRS):
        mixed = dot(hid[:, p * 256 : p * 256 + 512], b4f[...])
        sig = sigmoid(mixed)
        act = mixed * sig
        slope_mix[:, p * 256 : (p + 1) * 256] = (sig + act * (1.0 - sig)) * (1.0 / DATES)
        total = total + act
    embedded = ((total[:, 0:128] + total[:, 128:256]) * (1.0 / DATES)).astype(BF16)
    outgoing = dot(onehot[...], embedded)
    for d in DIRS:
        sum_send[d] = outgoing[d * P_OWN : (d + 1) * P_OWN].astype(BF16)
    start_all(sums_copy, DIRS)
    sums = outgoing[4 * P_OWN : 5 * P_OWN]
    for p in range(PAIRS):
        hid_t[p * 256 : (p + 1) * 256, :] = hid[:, 128 + p * 256 : 128 + (p + 1) * 256].T
    wait_recv_all(sums_copy, DIRS)
    for d in DIRS:
        sums = sums + sum_recv[d].astype(F32)

    centered = sums - jnp.mean(sums, axis=-1, keepdims=True)
    inverse = lax.rsqrt(jnp.mean(centered * centered, axis=-1, keepdims=True) + EPSILON)
    normed = centered * inverse
    rounded = normed.astype(BF16)
    kw = kw_ref[...]
    logits = dot(rounded, kw, ((1,), (1,)))
    exps = jnp.exp(logits)
    prob = exps / jnp.sum(exps, axis=-1, keepdims=True)
    lab = lab_ref[0]
    lab_col = jnp.sum(
        jnp.where(iota((P_OWN, P_OWN), 0) == iota((P_OWN, P_OWN), 1), lab.astype(F32), 0.0),
        axis=1,
        keepdims=True,
    ).astype(jnp.int32)
    hot = (lab_col == iota((P_OWN, CLASSES), 1)).astype(F32)
    g_logits = (prob - hot) * (1.0 / (P_OWN * n_row * n_col))
    g_normed = dot(g_logits, kw.astype(F32), ((1,), (0,)), PRECISE)
    g_parcel = inverse * (
        g_normed
        - jnp.mean(g_normed, axis=-1, keepdims=True)
        - normed * jnp.mean(g_normed * normed, axis=-1, keepdims=True)
    )
    g_parcel = g_parcel.astype(BF16)
    pgrad[...] = g_parcel
    start_all(grad_copy, DIRS)
    beside[4] = g_parcel
    class_term = dot(g_logits, rounded.astype(F32), ((0,), (0,)), PRECISE)
    wait_recv_all(grad_copy, DIRS)

    pixel_grad = dot(onehot_t[...], beside[...].reshape(SLOTS, C_OUT))
    pixel_grad = jnp.concatenate([pixel_grad, pixel_grad], axis=1)
    for p in range(PAIRS):
        gmix[:, 128 + p * 256 : 128 + (p + 1) * 256] = (
            pixel_grad * slope_mix[:, p * 256 : (p + 1) * 256]
        ).astype(BF16)
    for p in range(PAIRS):
        g_hid = dot(gmix[:, p * 256 : p * 256 + 512], b4b[...])
        g_pre = (g_hid * slope_pre[:, p * 256 : (p + 1) * 256]).astype(BF16)
        gpre[1 : T + 1, :, p * 256 : (p + 1) * 256] = g_pre.reshape(T, T, 256)
    start_all(row_copy, (1, 7))

    conv_t = None
    for p in range(PAIRS):
        g_pair = gpre[1 : T + 1, :, p * 256 : (p + 1) * 256].reshape(PIX, 256)
        term = dot(g_pair, taps(p), ((0,), (0,)))
        conv_t = term if conv_t is None else conv_t + term
    low_half = iota((128, 128), 1) < C_IN
    for t in range(9):
        both = jnp.where(
            low_half,
            conv_t[0:128, t * 128 : (t + 1) * 128],
            conv_t[128:256, t * 128 : (t + 1) * 128],
        ).T
        part[t * 64 : (t + 1) * 64, :] = (both[0:64] + both[64:128]).astype(BF16)
    even = None
    for p in range(PAIRS):
        term = dot(
            hid_t[p * 256 : (p + 1) * 256, :], gmix[:, 128 + p * 256 : 128 + (p + 1) * 256]
        )
        even = term if even is None else even + term
    odd = None
    for p in range(PAIRS - 1):
        term = dot(
            hid_t[p * 256 + 128 : p * 256 + 384, :],
            gmix[:, 256 + p * 256 : 512 + p * 256],
        )
        odd = term if odd is None else odd + term
    time_taps = (
        even[0:128, 128:256] + odd[0:128, 128:256],
        even[0:128, 0:128] + even[128:256, 128:256],
        even[128:256, 0:128] + odd[128:256, 0:128],
    )
    small = [
        jnp.sum(jnp.where(same_group, tap, 0.0).reshape(GROUPS, CPG, 128), axis=0)
        for tap in time_taps
    ]
    small.append(class_term)
    small.append(jnp.zeros((SMALL_ROWS - 3 * CPG - CLASSES, 128), F32))
    part[CONV_ROWS : CONV_ROWS + SMALL_ROWS, :] = jnp.concatenate(small, axis=0).astype(BF16)

    def shard_at(q):
        return pl.ds(pl.multiple_of(q * shard, 16), shard)

    def rs_copy(k):
        q, dev = a_dev(k)
        return pltpu.make_async_remote_copy(
            src_ref=part.at[shard_at(q)],
            dst_ref=rs_recv.at[k],
            send_sem=rs_ss.at[k],
            recv_sem=rs_rs.at[k],
            device_id=dev,
            device_id_type=MESH,
        )

    def bx_copy(k):
        return pltpu.make_async_remote_copy(
            src_ref=bx_recv.at[base],
            dst_ref=bx_recv.at[base],
            send_sem=bx_ss.at[k],
            recv_sem=bx_rs.at[k],
            device_id=b_dev(k),
            device_id_type=MESH,
        )

    def ag_copy(k):
        return pltpu.make_async_remote_copy(
            src_ref=final.at[shard_at(a_me)],
            dst_ref=final.at[shard_at(a_me)],
            send_sem=ag_ss.at[k],
            recv_sem=ag_rs.at[k],
            device_id=a_dev(k)[1],
            device_id_type=MESH,
        )

    for k in range(1, n_a):
        rs_copy(k).start()

    wait_recv_all(row_copy, (1, 7))
    j_at = lax.rem(iota((PIX, 128), 0), T)
    for p in range(PAIRS):
        g_rows = jnp.concatenate(
            [
                gpre[2 - r : 2 - r + T, :, p * 256 : (p + 1) * 256].reshape(PIX, 256)
                for r in range(3)
            ],
            axis=1,
        )
        z = dot(g_rows, wb[...])
        zs[0] = z[:, 0:128]
        zs[1] = z[:, 128:256]
        z_send[0, :, p * 128 : (p + 1) * 128] = zs[0, pl.ds(0, T, stride=T), :].astype(BF16)
        z_send[1, :, p * 128 : (p + 1) * 128] = zs[1, pl.ds(T - 1, T, stride=T), :].astype(BF16)
        from_right = jnp.where(j_at == T - 1, 0.0, pltpu.roll(z[:, 0:128], PIX - 1, 0))
        from_left = jnp.where(j_at == 0, 0.0, pltpu.roll(z[:, 128:256], 1, 0))
        zacc[p] = z[:, 256:384] + from_right + from_left
    start_all(col_copy, (3, 5))

    mine = part[shard_at(a_me)].astype(F32)
    for k in range(1, n_a):
        rs_copy(k).wait_recv()
    for k in range(1, n_a):
        mine = mine + rs_recv[k].astype(F32)
    bx_recv[base] = mine.astype(BF16)
    for k in range(1, n_b):
        bx_copy(k).start()

    wait_recv_all(col_copy, (3, 5))
    for p in range(PAIRS):
        lanes = slice(p * 128, (p + 1) * 128)
        at_left = zacc[p, pl.ds(0, T, stride=T), :] + z_recv[0, :, lanes].astype(F32)
        zacc[p, pl.ds(0, T, stride=T), :] = at_left
        at_right = zacc[p, pl.ds(T - 1, T, stride=T), :] + z_recv[1, :, lanes].astype(F32)
        zacc[p, pl.ds(T - 1, T, stride=T), :] = at_right
        gx_ref[:, :, lanes] = zacc[p].astype(BF16).reshape(T, T, 128)

    gx_store = pltpu.make_async_copy(gx_ref, gx_hbm, out_sems.at[0])
    gx_store.start()
    for k in range(1, n_b):
        pltpu.make_async_remote_copy(
            src_ref=bx_recv.at[base],
            dst_ref=bx_recv.at[lax.rem(base + n_b - k, n_b)],
            send_sem=bx_ss.at[k],
            recv_sem=bx_rs.at[k],
            device_id=b_dev(k),
            device_id_type=MESH,
        ).wait_recv()
    whole = bx_recv[0].astype(F32)
    for g in range(1, n_b):
        whole = whole + bx_recv[g].astype(F32)
    final[shard_at(a_me)] = whole.astype(BF16)
    for k in range(1, n_a):
        ag_copy(k).start()
    wait_send_all(pixel_copy, DIRS)
    wait_send_all(sums_copy, DIRS)
    wait_send_all(grad_copy, DIRS)
    wait_send_all(row_copy, (1, 7))
    wait_send_all(col_copy, (3, 5))
    for k in range(1, n_a):
        rs_copy(k).wait_send()
    for k in range(1, n_b):
        bx_copy(k).wait_send()
    for k in range(1, n_a):
        q = lax.rem(a_me + n_a - k, n_a)
        pltpu.make_async_remote_copy(
            src_ref=final.at[shard_at(a_me)],
            dst_ref=final.at[shard_at(q)],
            send_sem=ag_ss.at[k],
            recv_sem=ag_rs.at[k],
            device_id=a_dev(k)[1],
            device_id_type=MESH,
        ).wait_recv()
    final_store = pltpu.make_async_copy(final, final_hbm, out_sems.at[1])
    final_store.start()
    for k in range(1, n_a):
        ag_copy(k).wait_send()
    gx_store.wait()
    final_store.wait()


def finish(
    gx_in, final_in, gx_out, gcw_out, gtw_out, gkw_out,
    held, final, gcw_ref, gtw_ref, gkw_ref, in_sems, out_sems,
):
    rows = T // CHUNKS
    parts = [pl.ds(i * rows, rows) for i in range(CHUNKS)]
    loads = [
        pltpu.make_async_copy(gx_in.at[at], held.at[at], in_sems.at[i])
        for i, at in enumerate(parts)
    ]
    stores = [
        pltpu.make_async_copy(held.at[at], gx_out.at[at], out_sems.at[i])
        for i, at in enumerate(parts)
    ]
    for i, (src, dst) in enumerate(((gcw_ref, gcw_out), (gtw_ref, gtw_out), (gkw_ref, gkw_out))):
        stores.append(pltpu.make_async_copy(src, dst, out_sems.at[CHUNKS + i]))
    final_load = pltpu.make_async_copy(final_in, final, in_sems.at[CHUNKS])
    final_load.start()
    for load in loads:
        load.start()
    final_load.wait()
    for t in range(9):
        gcw_ref[t // 3, t % 3] = final[t * 64 : (t + 1) * 64, :].astype(F32)
    stores[CHUNKS].start()
    for load, store in zip(loads, stores):
        load.wait()
        store.start()
    width = 3 * CPG * CPG
    small = final[CONV_ROWS : CONV_ROWS + SMALL_ROWS, :]
    repeat = (lax.div(iota((width, SMALL_ROWS), 0), CPG) == iota((width, SMALL_ROWS), 1)).astype(
        BF16
    )
    rows = dot(repeat, small)
    own_out = lax.rem(iota((width, 128), 0), CPG) == lax.rem(iota((width, 128), 1), CPG)
    fold = (lax.div(iota((128, GROUPS), 0), CPG) == iota((128, GROUPS), 1)).astype(BF16)
    rows = jnp.where(own_out, rows, 0.0).astype(BF16)
    gtw_ref[...] = dot(rows, fold).reshape(3, CPG, CPG, GROUPS)
    gkw_ref[...] = small[3 * CPG : 3 * CPG + CLASSES].astype(F32)
    stores[CHUNKS + 1].start()
    stores[CHUNKS + 2].start()
    for store in stores:
        store.wait()


def per_device(n_row, n_col, pixels, conv_weight, time_weight, class_weight, *rest):
    args = (pixels, conv_weight, time_weight.transpose(0, 2, 3, 1), class_weight.T, *rest)
    n_a = 2 * n_col
    n_b = n_row // 2
    rows = CONV_ROWS + SMALL_ROWS
    shard = -(-rows // (16 * n_a)) * 16
    total = shard * n_a
    dma = pltpu.SemaphoreType.DMA
    anywhere = pl.BlockSpec(memory_space=pl.ANY)
    gx, final = pl.pallas_call(
        functools.partial(kernel, n_row, n_col, shard),
        out_shape=(
            jax.ShapeDtypeStruct((T, T, LX), BF16),
            jax.ShapeDtypeStruct((total, 128), BF16),
        ),
        in_specs=[anywhere] * 8,
        out_specs=(anywhere,) * 2,
        scratch_shapes=[
            pltpu.VMEM((T, T, LX), BF16),
            pltpu.VMEM((total, 128), BF16),
            dma((2,)),
            *[pltpu.VMEM(arg.shape, arg.dtype) for arg in args],
            dma((8,)),
            pltpu.VMEM((PAIRS, PIX, 128), F32),
            pltpu.VMEM((2, PAIRS, PIX + 2 * T, 128), F32),
            pltpu.VMEM((3, T + 2, T, LX), BF16),
            pltpu.VMEM((9 * 128, 256), BF16),
            pltpu.VMEM((3 * 256, 3 * 128), BF16),
            pltpu.VMEM((512, 256), BF16),
            pltpu.VMEM((512, 256), BF16),
            pltpu.VMEM((SLOTS, PIX), BF16),
            pltpu.VMEM((PIX, SLOTS), BF16),
            pltpu.VMEM((PIX, LG + 256), BF16),
            pltpu.VMEM((PIX, LG + 256), BF16),
            pltpu.VMEM((LG, PIX), BF16),
            pltpu.VMEM((PIX, LG), F32),
            pltpu.VMEM((PIX, LG), F32),
            pltpu.VMEM((T + 2, T, LG), BF16),
            pltpu.VMEM((2, PIX, 128), F32),
            pltpu.VMEM((PAIRS, PIX, 128), F32),
            pltpu.VMEM((2, T, LX), BF16),
            pltpu.VMEM((2, T, LX), BF16),
            pltpu.VMEM((4, T, 128), BF16),
            pltpu.VMEM((4, T, 128), BF16),
            pltpu.VMEM((9, P_OWN, C_OUT), BF16),
            pltpu.VMEM((9, P_OWN, C_OUT), BF16),
            pltpu.VMEM((P_OWN, C_OUT), BF16),
            pltpu.VMEM((9, P_OWN, C_OUT), BF16),
            pltpu.VMEM((2, T, LX), BF16),
            pltpu.VMEM((2, T, LX), BF16),
            pltpu.VMEM((total, 128), BF16),
            pltpu.VMEM((n_a, shard, 128), BF16),
            pltpu.VMEM((n_b, shard, 128), BF16),
            dma((9,)),
            dma((9,)),
            dma((9,)),
            dma((9,)),
            dma((9,)),
            dma((9,)),
            dma((2,)),
            dma((2,)),
            dma((2,)),
            dma((2,)),
            dma((n_a,)),
            dma((n_a,)),
            dma((n_b,)),
            dma((n_b,)),
            dma((n_a,)),
            dma((n_a,)),
        ],
        compiler_params=pltpu.CompilerParams(
            collective_id=0, has_side_effects=True, vmem_limit_bytes=VMEM_GRANT
        ),
    )(*args)
    gx, conv_grad, time_grad, class_grad = pl.pallas_call(
        finish,
        out_shape=(
            jax.ShapeDtypeStruct((T, T, LX), BF16),
            jax.ShapeDtypeStruct((3, 3, C_IN, C_OUT), F32),
            jax.ShapeDtypeStruct((3, CPG, CPG, GROUPS), F32),
            jax.ShapeDtypeStruct((CLASSES, C_OUT), F32),
        ),
        in_specs=[anywhere] * 2,
        out_specs=(anywhere,) * 4,
        scratch_shapes=[
            pltpu.VMEM((T, T, LX), BF16),
            pltpu.VMEM((total, 128), BF16),
            pltpu.VMEM((3, 3, C_IN, C_OUT), F32),
            pltpu.VMEM((3, CPG, CPG, GROUPS), F32),
            pltpu.VMEM((CLASSES, C_OUT), F32),
            dma((CHUNKS + 1,)),
            dma((CHUNKS + 3,)),
        ],
        compiler_params=pltpu.CompilerParams(vmem_limit_bytes=VMEM_GRANT),
    )(gx, final)
    return gx, conv_grad, time_grad.transpose(0, 3, 1, 2), class_grad.T


def solution(mesh):
    in_specs = (
        P("row", "col", None),
        P(),
        P(),
        P(),
        P("row", "col"),
        P("row", "col", None),
        P("row", "col", None),
        P("row", "col", None),
    )
    out_specs = (P("row", "col", None), P(), P(), P())
    return jax.shard_map(
        functools.partial(per_device, mesh.shape["row"], mesh.shape["col"]),
        mesh=mesh,
        in_specs=in_specs,
        out_specs=out_specs,
        check_vma=False,
    )
```

```python
import functools

import jax
import jax.numpy as jnp
from jax import lax
from jax.experimental import pallas as pl
from jax.experimental.pallas import tpu as pltpu
from jax.sharding import PartitionSpec as P

DATES = 12
C_IN = 64
C_OUT = 128
GROUPS = 16
CLASSES = 20
P_OWN = 32
S_STR = 32
CPG = 8
EPSILON = 1e-05
PRECISE = lax.Precision.HIGHEST
MESH = pl.DeviceIdType.MESH
F32 = jnp.float32
BF16 = jnp.bfloat16

VMEM_GRANT = 63 * 1024 * 1024
CHUNKS = 4
T = 16
PIX = T * T
PAIRS = DATES // 2
LX = DATES * C_IN
LG = DATES * C_OUT
SLOTS = 9 * P_OWN
CONV_ROWS = 9 * C_IN
SMALL_ROWS = 48
DIRS = [d for d in range(9) if d != 4]


def iota(shape, dim):
    return lax.broadcasted_iota(jnp.int32, shape, dim)


def dot(a, b, dims=((1,), (0,)), precision=None):
    return lax.dot_general(
        a, b, (dims, ((), ())), preferred_element_type=F32, precision=precision
    )


def sigmoid(v):
    return 0.5 * jnp.tanh(0.5 * v) + 0.5


def kernel(
    n_row,
    n_col,
    shard,
    x_hbm,
    cw_hbm,
    tw_hbm,
    kw_hbm,
    slot_hbm,
    sdir_hbm,
    sslot_hbm,
    lab_hbm,
    gx_hbm,
    final_hbm,
    gx_ref,
    final,
    out_sems,
    x_ref,
    cw_ref,
    tw_ref,
    kw_ref,
    slot_ref,
    sdir_ref,
    sslot_ref,
    lab_ref,
    in_sems,
    xf,
    xs,
    xc,
    wf,
    wb,
    b4f,
    b4b,
    onehot,
    onehot_t,
    hid,
    gmix,
    hid_t,
    slope_pre,
    slope_mix,
    gpre,
    zs,
    zacc,
    col_send,
    col_recv,
    cor_send,
    cor_recv,
    sum_send,
    sum_recv,
    pgrad,
    beside,
    z_send,
    z_recv,
    part,
    rs_recv,
    bx_recv,
    px_ss,
    px_rs,
    ps_ss,
    ps_rs,
    pg_ss,
    pg_rs,
    gh_ss,
    gh_rs,
    zc_ss,
    zc_rs,
    rs_ss,
    rs_rs,
    bx_ss,
    bx_rs,
    ag_ss,
    ag_rs,
):
    row = lax.axis_index("row")
    col = lax.axis_index("col")
    n_a = 2 * n_col
    n_b = n_row // 2
    base = lax.div(row, 2)
    a_row = lax.rem(row, 2)
    a_me = a_row * n_col + col

    def a_dev(k):
        q = lax.rem(a_me + k, n_a)
        return q, (base * 2 + lax.div(q, n_col), lax.rem(q, n_col))

    def b_dev(k):
        return (lax.rem(base + k, n_b) * 2 + a_row, col)

    def neighbour(d):
        r = row + (d // 3 - 1)
        c = col + (d % 3 - 1)
        there = (r >= 0) & (r < n_row) & (c >= 0) & (c < n_col)
        return there, (r, c)

    fetches = [
        pltpu.make_async_copy(src, dst, in_sems.at[i])
        for i, (src, dst) in enumerate(
            (
                (x_hbm, x_ref),
                (cw_hbm, cw_ref),
                (tw_hbm, tw_ref),
                (kw_hbm, kw_ref),
                (slot_hbm, slot_ref),
                (sdir_hbm, sdir_ref),
                (sslot_hbm, sslot_ref),
                (lab_hbm, lab_ref),
            )
        )
    ]
    for fetch in fetches:
        fetch.start()

    xc[1, 0] = jnp.zeros((T, LX), BF16)
    xc[1, T + 1] = jnp.zeros((T, LX), BF16)
    gpre[0] = jnp.zeros((T, LG), BF16)
    gpre[T + 1] = jnp.zeros((T, LG), BF16)
    col_recv[...] = jnp.zeros(col_recv.shape, BF16)
    cor_recv[...] = jnp.zeros(cor_recv.shape, BF16)
    sum_recv[...] = jnp.zeros(sum_recv.shape, BF16)
    beside[...] = jnp.zeros(beside.shape, BF16)
    z_recv[...] = jnp.zeros(z_recv.shape, BF16)

    barrier = pltpu.get_barrier_semaphore()
    expected = n_a - 1 + n_b - 1
    for d in DIRS:
        there, dev = neighbour(d)
        expected = expected + there.astype(jnp.int32)

        @pl.when(there)
        def _():
            pl.semaphore_signal(barrier, inc=1, device_id=dev, device_id_type=MESH)

    for k in range(1, n_a):
        pl.semaphore_signal(barrier, inc=1, device_id=a_dev(k)[1], device_id_type=MESH)
    for k in range(1, n_b):
        pl.semaphore_signal(barrier, inc=1, device_id=b_dev(k), device_id_type=MESH)

    fetches[0].wait()
    x_own = x_ref[...].astype(F32).reshape(PIX, LX)
    left, right = [], []
    for p in range(PAIRS):
        xf[p] = x_own[:, p * 128 : (p + 1) * 128]
        left.append(xf[p, pl.ds(0, T, stride=T), :])
        right.append(xf[p, pl.ds(T - 1, T, stride=T), :])
        col_send[0, :, p * 128 : (p + 1) * 128] = left[p].astype(BF16)
        col_send[1, :, p * 128 : (p + 1) * 128] = right[p].astype(BF16)
    which = iota((T, 128), 0)
    for corner, source, at in ((0, left, 0), (1, right, 0), (2, left, T - 1), (3, right, T - 1)):
        block = jnp.zeros((T, 128), F32)
        for p in range(PAIRS):
            piece = source[p][at : at + 1, :]
            block = jnp.where(which == p, jnp.broadcast_to(piece, (T, 128)), block)
        cor_send[corner] = block.astype(BF16)

    pl.semaphore_wait(barrier, expected)

    corner_of = {0: 0, 2: 1, 6: 2, 8: 3}

    def pixel_copy(d, dev):
        o = 8 - d
        if d in corner_of:
            src, dst = cor_send.at[corner_of[d]], cor_recv.at[corner_of[o]]
        elif d == 1:
            src, dst = x_ref.at[0], xc.at[1, T + 1]
        elif d == 7:
            src, dst = x_ref.at[T - 1], xc.at[1, 0]
        elif d == 3:
            src, dst = col_send.at[0], col_recv.at[1]
        else:
            src, dst = col_send.at[1], col_recv.at[0]
        return pltpu.make_async_remote_copy(
            src_ref=src,
            dst_ref=dst,
            send_sem=px_ss.at[d],
            recv_sem=px_rs.at[o],
            device_id=dev,
            device_id_type=MESH,
        )

    def sums_copy(d, dev):
        return pltpu.make_async_remote_copy(
            src_ref=sum_send.at[d],
            dst_ref=sum_recv.at[8 - d],
            send_sem=ps_ss.at[d],
            recv_sem=ps_rs.at[8 - d],
            device_id=dev,
            device_id_type=MESH,
        )

    def grad_copy(d, dev):
        return pltpu.make_async_remote_copy(
            src_ref=pgrad,
            dst_ref=beside.at[8 - d],
            send_sem=pg_ss.at[d],
            recv_sem=pg_rs.at[8 - d],
            device_id=dev,
            device_id_type=MESH,
        )

    def row_copy(d, dev):
        k = 0 if d == 1 else 1
        return pltpu.make_async_remote_copy(
            src_ref=gpre.at[1 if d == 1 else T],
            dst_ref=gpre.at[T + 1 if d == 1 else 0],
            send_sem=gh_ss.at[k],
            recv_sem=gh_rs.at[1 - k],
            device_id=dev,
            device_id_type=MESH,
        )

    def col_copy(d, dev):
        k = 0 if d == 3 else 1
        return pltpu.make_async_remote_copy(
            src_ref=z_send.at[k],
            dst_ref=z_recv.at[1 - k],
            send_sem=zc_ss.at[k],
            recv_sem=zc_rs.at[1 - k],
            device_id=dev,
            device_id_type=MESH,
        )

    def start_all(make, dirs):
        for d in dirs:
            there, dev = neighbour(d)

            @pl.when(there)
            def _():
                make(d, dev).start()

    def wait_recv_all(make, dirs):
        for d in dirs:
            there, dev = neighbour(d)

            @pl.when(there)
            def _():
                make(8 - d, dev).wait_recv()

    def wait_send_all(make, dirs):
        for d in dirs:
            there, dev = neighbour(d)

            @pl.when(there)
            def _():
                make(d, dev).wait_send()

    start_all(pixel_copy, DIRS)

    for fetch in fetches[1:]:
        fetch.wait()
    xc[1, 1 : T + 1] = x_ref[...]
    wf[...] = jnp.zeros(wf.shape, BF16)
    for r in range(3):
        for c in range(3):
            t = r * 3 + c
            w = cw_ref[r, c]
            wf[t * 128 : t * 128 + 64, 0:128] = w
            wf[t * 128 + 64 : t * 128 + 128, 128:256] = w
    for r in range(3):
        for slot_at, c in ((0, 0), (1, 2), (2, 1)):
            t = r * 3 + c
            block = wf[t * 128 : (t + 1) * 128, :].astype(F32)
            wb[r * 256 : (r + 1) * 256, slot_at * 128 : (slot_at + 1) * 128] = block.T.astype(BF16)
    same_group = lax.div(iota((128, 128), 0), CPG) == lax.div(iota((128, 128), 1), CPG)
    width = 3 * CPG * CPG
    by_group = (lax.div(iota((128, GROUPS), 0), CPG) == iota((128, GROUPS), 1)).astype(BF16)
    compact = tw_ref[...].astype(F32).reshape(width, GROUPS).astype(BF16)
    spread_rows = dot(by_group, compact, ((1,), (1,)))
    entry = iota((128, width), 1)
    in_chan = lax.rem(iota((128, width), 0), CPG)
    fold_out = (
        lax.rem(iota((width, 128), 0), CPG) == lax.rem(iota((width, 128), 1), CPG)
    ).astype(BF16)
    dense, dense_t = [], []
    for tap in range(3):
        rows = jnp.where(lax.div(entry, CPG) == tap * CPG + in_chan, spread_rows, 0.0)
        d_tap = jnp.where(same_group, dot(rows.astype(BF16), fold_out), 0.0)
        dense.append(d_tap.astype(BF16))
        dense_t.append(d_tap.T.astype(BF16))
    nothing = jnp.zeros((128, 128), BF16)
    for ref, (one, two, three) in ((b4f, dense), (b4b, dense_t[::-1])):
        for i, (lo, hi) in enumerate(((one, nothing), (two, one), (three, two), (nothing, three))):
            ref[i * 128 : (i + 1) * 128, 0:128] = lo
            ref[i * 128 : (i + 1) * 128, 128:256] = hi
    zero_side = jnp.zeros((PIX, 128), BF16)
    hid[:, 0:128] = zero_side
    hid[:, 128 + LG : 256 + LG] = zero_side
    gmix[:, 0:128] = zero_side
    gmix[:, 128 + LG : 256 + LG] = zero_side

    pick_row = (lax.div(iota((PIX, T), 0), T) == iota((PIX, T), 1)).astype(BF16)
    by_row = dot(pick_row, slot_ref[...].astype(F32).astype(BF16))
    at_col = lax.rem(iota((PIX, T), 0), T) == iota((PIX, T), 1)
    slot_of = jnp.sum(jnp.where(at_col, by_row, 0.0), axis=1, keepdims=True).astype(jnp.int32)
    in_own = (slot_of == iota((PIX, P_OWN), 1)).astype(BF16)
    in_str = (slot_of - P_OWN == iota((PIX, S_STR), 1)).astype(BF16)
    target = sdir_ref[0] * P_OWN + sslot_ref[0]
    sel_own = (iota((SLOTS, P_OWN), 0) == iota((SLOTS, P_OWN), 1) + 4 * P_OWN).astype(BF16)
    sel_str = (iota((SLOTS, S_STR), 0) == target).astype(BF16)
    onehot[...] = (
        dot(sel_own, in_own, ((1,), (1,))) + dot(sel_str, in_str, ((1,), (1,)))
    ).astype(BF16)
    onehot_t[...] = (
        dot(in_own, sel_own, ((1,), (1,))) + dot(in_str, sel_str, ((1,), (1,)))
    ).astype(BF16)

    for p in range(PAIRS):
        lanes = x_own[:, p * 128 : (p + 1) * 128]
        xs[0, p, T : T + PIX] = pltpu.roll(lanes, 1, 0)
        xs[1, p, T : T + PIX] = pltpu.roll(lanes, PIX - 1, 0)
    wait_recv_all(pixel_copy, DIRS)
    for halo in (0, T + 1):
        line = xc[1, halo].astype(F32)
        for p in range(PAIRS):
            lanes = line[:, p * 128 : (p + 1) * 128]
            xs[0, p, halo * T : (halo + 1) * T] = pltpu.roll(lanes, 1, 0)
            xs[1, p, halo * T : (halo + 1) * T] = pltpu.roll(lanes, T - 1, 0)
    for side, at in ((0, 0), (1, T - 1)):
        arrived = col_recv[side].astype(F32)
        top = cor_recv[side].astype(F32)
        bottom = cor_recv[2 + side].astype(F32)
        last = (T + 1) * T
        for p in range(PAIRS):
            lanes = slice(p * 128, (p + 1) * 128)
            xs[side, p, pl.ds(T + at, T, stride=T), :] = arrived[:, lanes]
            xs[side, p, at : at + 1, :] = top[p : p + 1, :]
            xs[side, p, last + at : last + at + 1, :] = bottom[p : p + 1, :]
            xc[2 * side, :, :, lanes] = xs[side, p].astype(BF16).reshape(T + 2, T, 128)

    def taps(p):
        return jnp.concatenate(
            [
                xc[c, r : r + T, :, p * 128 : (p + 1) * 128].reshape(PIX, 128)
                for r in range(3)
                for c in range(3)
            ],
            axis=1,
        )

    for p in range(PAIRS):
        pre = dot(taps(p), wf[...])
        sig = sigmoid(pre)
        act = pre * sig
        slope_pre[:, p * 256 : (p + 1) * 256] = sig + act * (1.0 - sig)
        hid[:, 128 + p * 256 : 128 + (p + 1) * 256] = act.astype(BF16)
    total = jnp.zeros((PIX, 256), F32)
    for p in range(PAIRS):
        mixed = dot(hid[:, p * 256 : p * 256 + 512], b4f[...])
        sig = sigmoid(mixed)
        act = mixed * sig
        slope_mix[:, p * 256 : (p + 1) * 256] = (sig + act * (1.0 - sig)) * (1.0 / DATES)
        total = total + act
    embedded = ((total[:, 0:128] + total[:, 128:256]) * (1.0 / DATES)).astype(BF16)
    outgoing = dot(onehot[...], embedded)
    for d in DIRS:
        sum_send[d] = outgoing[d * P_OWN : (d + 1) * P_OWN].astype(BF16)
    start_all(sums_copy, DIRS)
    sums = outgoing[4 * P_OWN : 5 * P_OWN]
    for p in range(PAIRS):
        hid_t[p * 256 : (p + 1) * 256, :] = hid[:, 128 + p * 256 : 128 + (p + 1) * 256].T
    wait_recv_all(sums_copy, DIRS)
    for d in DIRS:
        sums = sums + sum_recv[d].astype(F32)

    centered = sums - jnp.mean(sums, axis=-1, keepdims=True)
    inverse = lax.rsqrt(jnp.mean(centered * centered, axis=-1, keepdims=True) + EPSILON)
    normed = centered * inverse
    rounded = normed.astype(BF16)
    kw = kw_ref[...]
    logits = dot(rounded, kw, ((1,), (1,)))
    exps = jnp.exp(logits)
    prob = exps / jnp.sum(exps, axis=-1, keepdims=True)
    lab = lab_ref[0]
    lab_col = jnp.sum(
        jnp.where(iota((P_OWN, P_OWN), 0) == iota((P_OWN, P_OWN), 1), lab.astype(F32), 0.0),
        axis=1,
        keepdims=True,
    ).astype(jnp.int32)
    hot = (lab_col == iota((P_OWN, CLASSES), 1)).astype(F32)
    g_logits = (prob - hot) * (1.0 / (P_OWN * n_row * n_col))
    g_normed = dot(g_logits, kw.astype(F32), ((1,), (0,)), PRECISE)
    g_parcel = inverse * (
        g_normed
        - jnp.mean(g_normed, axis=-1, keepdims=True)
        - normed * jnp.mean(g_normed * normed, axis=-1, keepdims=True)
    )
    g_parcel = g_parcel.astype(BF16)
    pgrad[...] = g_parcel
    start_all(grad_copy, DIRS)
    beside[4] = g_parcel
    class_term = dot(g_logits, rounded.astype(F32), ((0,), (0,)), PRECISE)
    wait_recv_all(grad_copy, DIRS)

    pixel_grad = dot(onehot_t[...], beside[...].reshape(SLOTS, C_OUT))
    pixel_grad = jnp.concatenate([pixel_grad, pixel_grad], axis=1)
    for p in range(PAIRS):
        gmix[:, 128 + p * 256 : 128 + (p + 1) * 256] = (
            pixel_grad * slope_mix[:, p * 256 : (p + 1) * 256]
        ).astype(BF16)
    for p in range(PAIRS):
        g_hid = dot(gmix[:, p * 256 : p * 256 + 512], b4b[...])
        g_pre = (g_hid * slope_pre[:, p * 256 : (p + 1) * 256]).astype(BF16)
        gpre[1 : T + 1, :, p * 256 : (p + 1) * 256] = g_pre.reshape(T, T, 256)
    start_all(row_copy, (1, 7))

    g_all = jnp.concatenate(
        [
            gpre[1 : T + 1, :, p * 256 : (p + 1) * 256].reshape(PIX, 256)
            for p in range(PAIRS)
        ],
        axis=0,
    )
    conv_t = dot(g_all, jnp.concatenate([taps(p) for p in range(PAIRS)], axis=0), ((0,), (0,)))
    low_half = iota((128, 128), 1) < C_IN
    for t in range(9):
        both = jnp.where(
            low_half,
            conv_t[0:128, t * 128 : (t + 1) * 128],
            conv_t[128:256, t * 128 : (t + 1) * 128],
        ).T
        part[t * 64 : (t + 1) * 64, :] = (both[0:64] + both[64:128]).astype(BF16)
    even = None
    for p in range(PAIRS):
        term = dot(
            hid_t[p * 256 : (p + 1) * 256, :], gmix[:, 128 + p * 256 : 128 + (p + 1) * 256]
        )
        even = term if even is None else even + term
    odd = None
    for p in range(PAIRS - 1):
        term = dot(
            hid_t[p * 256 + 128 : p * 256 + 384, :],
            gmix[:, 256 + p * 256 : 512 + p * 256],
        )
        odd = term if odd is None else odd + term
    time_taps = (
        even[0:128, 128:256] + odd[0:128, 128:256],
        even[0:128, 0:128] + even[128:256, 128:256],
        even[128:256, 0:128] + odd[128:256, 0:128],
    )
    small = [
        jnp.sum(jnp.where(same_group, tap, 0.0).reshape(GROUPS, CPG, 128), axis=0)
        for tap in time_taps
    ]
    small.append(class_term)
    small.append(jnp.zeros((SMALL_ROWS - 3 * CPG - CLASSES, 128), F32))
    part[CONV_ROWS : CONV_ROWS + SMALL_ROWS, :] = jnp.concatenate(small, axis=0).astype(BF16)

    def shard_at(q):
        return pl.ds(pl.multiple_of(q * shard, 16), shard)

    def rs_copy(k):
        q, dev = a_dev(k)
        return pltpu.make_async_remote_copy(
            src_ref=part.at[shard_at(q)],
            dst_ref=rs_recv.at[k],
            send_sem=rs_ss.at[k],
            recv_sem=rs_rs.at[k],
            device_id=dev,
            device_id_type=MESH,
        )

    def bx_copy(k):
        return pltpu.make_async_remote_copy(
            src_ref=bx_recv.at[base],
            dst_ref=bx_recv.at[base],
            send_sem=bx_ss.at[k],
            recv_sem=bx_rs.at[k],
            device_id=b_dev(k),
            device_id_type=MESH,
        )

    def ag_copy(k):
        return pltpu.make_async_remote_copy(
            src_ref=final.at[shard_at(a_me)],
            dst_ref=final.at[shard_at(a_me)],
            send_sem=ag_ss.at[k],
            recv_sem=ag_rs.at[k],
            device_id=a_dev(k)[1],
            device_id_type=MESH,
        )

    for k in range(1, n_a):
        rs_copy(k).start()

    wait_recv_all(row_copy, (1, 7))
    j_at = lax.rem(iota((PIX, 128), 0), T)
    for p in range(PAIRS):
        g_rows = jnp.concatenate(
            [
                gpre[2 - r : 2 - r + T, :, p * 256 : (p + 1) * 256].reshape(PIX, 256)
                for r in range(3)
            ],
            axis=1,
        )
        z = dot(g_rows, wb[...])
        zs[0] = z[:, 0:128]
        zs[1] = z[:, 128:256]
        z_send[0, :, p * 128 : (p + 1) * 128] = zs[0, pl.ds(0, T, stride=T), :].astype(BF16)
        z_send[1, :, p * 128 : (p + 1) * 128] = zs[1, pl.ds(T - 1, T, stride=T), :].astype(BF16)
        from_right = jnp.where(j_at == T - 1, 0.0, pltpu.roll(z[:, 0:128], PIX - 1, 0))
        from_left = jnp.where(j_at == 0, 0.0, pltpu.roll(z[:, 128:256], 1, 0))
        zacc[p] = z[:, 256:384] + from_right + from_left
    start_all(col_copy, (3, 5))

    mine = part[shard_at(a_me)].astype(F32)
    for k in range(1, n_a):
        rs_copy(k).wait_recv()
    for k in range(1, n_a):
        mine = mine + rs_recv[k].astype(F32)
    bx_recv[base] = mine.astype(BF16)
    for k in range(1, n_b):
        bx_copy(k).start()

    wait_recv_all(col_copy, (3, 5))
    for p in range(PAIRS):
        lanes = slice(p * 128, (p + 1) * 128)
        at_left = zacc[p, pl.ds(0, T, stride=T), :] + z_recv[0, :, lanes].astype(F32)
        zacc[p, pl.ds(0, T, stride=T), :] = at_left
        at_right = zacc[p, pl.ds(T - 1, T, stride=T), :] + z_recv[1, :, lanes].astype(F32)
        zacc[p, pl.ds(T - 1, T, stride=T), :] = at_right
        gx_ref[:, :, lanes] = zacc[p].astype(BF16).reshape(T, T, 128)

    gx_store = pltpu.make_async_copy(gx_ref, gx_hbm, out_sems.at[0])
    gx_store.start()
    for k in range(1, n_b):
        pltpu.make_async_remote_copy(
            src_ref=bx_recv.at[base],
            dst_ref=bx_recv.at[lax.rem(base + n_b - k, n_b)],
            send_sem=bx_ss.at[k],
            recv_sem=bx_rs.at[k],
            device_id=b_dev(k),
            device_id_type=MESH,
        ).wait_recv()
    whole = bx_recv[0].astype(F32)
    for g in range(1, n_b):
        whole = whole + bx_recv[g].astype(F32)
    final[shard_at(a_me)] = whole.astype(BF16)
    for k in range(1, n_a):
        ag_copy(k).start()
    wait_send_all(pixel_copy, DIRS)
    wait_send_all(sums_copy, DIRS)
    wait_send_all(grad_copy, DIRS)
    wait_send_all(row_copy, (1, 7))
    wait_send_all(col_copy, (3, 5))
    for k in range(1, n_a):
        rs_copy(k).wait_send()
    for k in range(1, n_b):
        bx_copy(k).wait_send()
    for k in range(1, n_a):
        q = lax.rem(a_me + n_a - k, n_a)
        pltpu.make_async_remote_copy(
            src_ref=final.at[shard_at(a_me)],
            dst_ref=final.at[shard_at(q)],
            send_sem=ag_ss.at[k],
            recv_sem=ag_rs.at[k],
            device_id=a_dev(k)[1],
            device_id_type=MESH,
        ).wait_recv()
    final_store = pltpu.make_async_copy(final, final_hbm, out_sems.at[1])
    final_store.start()
    for k in range(1, n_a):
        ag_copy(k).wait_send()
    gx_store.wait()
    final_store.wait()


def finish(
    gx_in, final_in, gx_out, gcw_out, gtw_out, gkw_out,
    held, final, gcw_ref, gtw_ref, gkw_ref, in_sems, out_sems,
):
    rows = T // CHUNKS
    parts = [pl.ds(i * rows, rows) for i in range(CHUNKS)]
    loads = [
        pltpu.make_async_copy(gx_in.at[at], held.at[at], in_sems.at[i])
        for i, at in enumerate(parts)
    ]
    stores = [
        pltpu.make_async_copy(held.at[at], gx_out.at[at], out_sems.at[i])
        for i, at in enumerate(parts)
    ]
    for i, (src, dst) in enumerate(((gcw_ref, gcw_out), (gtw_ref, gtw_out), (gkw_ref, gkw_out))):
        stores.append(pltpu.make_async_copy(src, dst, out_sems.at[CHUNKS + i]))
    final_load = pltpu.make_async_copy(final_in, final, in_sems.at[CHUNKS])
    final_load.start()
    for load in loads:
        load.start()
    final_load.wait()
    for t in range(9):
        gcw_ref[t // 3, t % 3] = final[t * 64 : (t + 1) * 64, :].astype(F32)
    stores[CHUNKS].start()
    for load, store in zip(loads, stores):
        load.wait()
        store.start()
    width = 3 * CPG * CPG
    small = final[CONV_ROWS : CONV_ROWS + SMALL_ROWS, :]
    repeat = (lax.div(iota((width, SMALL_ROWS), 0), CPG) == iota((width, SMALL_ROWS), 1)).astype(
        BF16
    )
    rows = dot(repeat, small)
    own_out = lax.rem(iota((width, 128), 0), CPG) == lax.rem(iota((width, 128), 1), CPG)
    fold = (lax.div(iota((128, GROUPS), 0), CPG) == iota((128, GROUPS), 1)).astype(BF16)
    rows = jnp.where(own_out, rows, 0.0).astype(BF16)
    gtw_ref[...] = dot(rows, fold).reshape(3, CPG, CPG, GROUPS)
    gkw_ref[...] = small[3 * CPG : 3 * CPG + CLASSES].astype(F32)
    stores[CHUNKS + 1].start()
    stores[CHUNKS + 2].start()
    for store in stores:
        store.wait()


def per_device(n_row, n_col, pixels, conv_weight, time_weight, class_weight, *rest):
    args = (pixels, conv_weight, time_weight.transpose(0, 2, 3, 1), class_weight.T, *rest)
    n_a = 2 * n_col
    n_b = n_row // 2
    rows = CONV_ROWS + SMALL_ROWS
    shard = -(-rows // (16 * n_a)) * 16
    total = shard * n_a
    dma = pltpu.SemaphoreType.DMA
    anywhere = pl.BlockSpec(memory_space=pl.ANY)
    gx, final = pl.pallas_call(
        functools.partial(kernel, n_row, n_col, shard),
        out_shape=(
            jax.ShapeDtypeStruct((T, T, LX), BF16),
            jax.ShapeDtypeStruct((total, 128), BF16),
        ),
        in_specs=[anywhere] * 8,
        out_specs=(anywhere,) * 2,
        scratch_shapes=[
            pltpu.VMEM((T, T, LX), BF16),
            pltpu.VMEM((total, 128), BF16),
            dma((2,)),
            *[pltpu.VMEM(arg.shape, arg.dtype) for arg in args],
            dma((8,)),
            pltpu.VMEM((PAIRS, PIX, 128), F32),
            pltpu.VMEM((2, PAIRS, PIX + 2 * T, 128), F32),
            pltpu.VMEM((3, T + 2, T, LX), BF16),
            pltpu.VMEM((9 * 128, 256), BF16),
            pltpu.VMEM((3 * 256, 3 * 128), BF16),
            pltpu.VMEM((512, 256), BF16),
            pltpu.VMEM((512, 256), BF16),
            pltpu.VMEM((SLOTS, PIX), BF16),
            pltpu.VMEM((PIX, SLOTS), BF16),
            pltpu.VMEM((PIX, LG + 256), BF16),
            pltpu.VMEM((PIX, LG + 256), BF16),
            pltpu.VMEM((LG, PIX), BF16),
            pltpu.VMEM((PIX, LG), F32),
            pltpu.VMEM((PIX, LG), F32),
            pltpu.VMEM((T + 2, T, LG), BF16),
            pltpu.VMEM((2, PIX, 128), F32),
            pltpu.VMEM((PAIRS, PIX, 128), F32),
            pltpu.VMEM((2, T, LX), BF16),
            pltpu.VMEM((2, T, LX), BF16),
            pltpu.VMEM((4, T, 128), BF16),
            pltpu.VMEM((4, T, 128), BF16),
            pltpu.VMEM((9, P_OWN, C_OUT), BF16),
            pltpu.VMEM((9, P_OWN, C_OUT), BF16),
            pltpu.VMEM((P_OWN, C_OUT), BF16),
            pltpu.VMEM((9, P_OWN, C_OUT), BF16),
            pltpu.VMEM((2, T, LX), BF16),
            pltpu.VMEM((2, T, LX), BF16),
            pltpu.VMEM((total, 128), BF16),
            pltpu.VMEM((n_a, shard, 128), BF16),
            pltpu.VMEM((n_b, shard, 128), BF16),
            dma((9,)),
            dma((9,)),
            dma((9,)),
            dma((9,)),
            dma((9,)),
            dma((9,)),
            dma((2,)),
            dma((2,)),
            dma((2,)),
            dma((2,)),
            dma((n_a,)),
            dma((n_a,)),
            dma((n_b,)),
            dma((n_b,)),
            dma((n_a,)),
            dma((n_a,)),
        ],
        compiler_params=pltpu.CompilerParams(
            collective_id=0, has_side_effects=True, vmem_limit_bytes=VMEM_GRANT
        ),
    )(*args)
    gx, conv_grad, time_grad, class_grad = pl.pallas_call(
        finish,
        out_shape=(
            jax.ShapeDtypeStruct((T, T, LX), BF16),
            jax.ShapeDtypeStruct((3, 3, C_IN, C_OUT), F32),
            jax.ShapeDtypeStruct((3, CPG, CPG, GROUPS), F32),
            jax.ShapeDtypeStruct((CLASSES, C_OUT), F32),
        ),
        in_specs=[anywhere] * 2,
        out_specs=(anywhere,) * 4,
        scratch_shapes=[
            pltpu.VMEM((T, T, LX), BF16),
            pltpu.VMEM((total, 128), BF16),
            pltpu.VMEM((3, 3, C_IN, C_OUT), F32),
            pltpu.VMEM((3, CPG, CPG, GROUPS), F32),
            pltpu.VMEM((CLASSES, C_OUT), F32),
            dma((CHUNKS + 1,)),
            dma((CHUNKS + 3,)),
        ],
        compiler_params=pltpu.CompilerParams(vmem_limit_bytes=VMEM_GRANT),
    )(gx, final)
    return gx, conv_grad, time_grad.transpose(0, 3, 1, 2), class_grad.T


def solution(mesh):
    in_specs = (
        P("row", "col", None),
        P(),
        P(),
        P(),
        P("row", "col"),
        P("row", "col", None),
        P("row", "col", None),
        P("row", "col", None),
    )
    out_specs = (P("row", "col", None), P(), P(), P())
    return jax.shard_map(
        functools.partial(per_device, mesh.shape["row"], mesh.shape["col"]),
        mesh=mesh,
        in_specs=in_specs,
        out_specs=out_specs,
        check_vma=False,
    )
```
